256 devices in a mesh: dp: 64 (over z, y, x_hi), sy: 2 (over x_lo), sx: 2 (over core).
Axes of the slice: x: 4 (x_hi: 2, x_lo: 2; x = x_hi * 2 + x_lo), y: 4, z: 8, core: 2. Of those that a mesh axis runs over, the one named last changes fastest.
Arguments:
- features: bfloat16 [64, 56, 56, 256], P('dp', 'sy', 'sx'), may hold values from -8 to 8
- labels: int32 [64], P('dp'), may hold values from 0 to 999
- grid: int32 [2], replicated, may hold values from 0 to 49
- w_reduce: bfloat16 [3, 256, 64], P(None, None, 'dp'), may hold values from -0.375 to 0.375
- w_spatial: bfloat16 [3, 3, 3, 64, 64], P(None, None, None, None, 'dp'), may hold values from -0.25 to 0.25
- w_expand: bfloat16 [3, 64, 256], P(None, None, 'dp'), may hold values from -0.75 to 0.75
- w_class: bfloat16 [256, 1000], P('dp'), may hold values from -1.5 to 1.5
- dir_reduce: bfloat16 [2, 3, 256, 64], P(None, None, None, 'dp'), may hold values from -6 to 6
- dir_spatial: bfloat16 [2, 3, 3, 3, 64, 64], P(None, None, None, None, None, 'dp'), may hold values from -6 to 6
- dir_expand: bfloat16 [2, 3, 64, 256], P(None, None, None, 'dp'), may hold values from -6 to 6
- dir_class: bfloat16 [2, 256, 1000], P(None, 'dp'), may hold values from -6 to 6
- gain_mid: float32 [3, 2, 64], replicated, may hold values from 0.5 to 1.5
- shift_mid: float32 [3, 2, 64], replicated, may hold values from -3 to 3
- gain_out: float32 [3, 256], replicated, may hold values from 0.5 to 1.5
- shift_out: float32 [3, 256], replicated, may hold values from -3 to 3
Outputs:
- section_out: bfloat16 [64, 56, 56, 256], P('dp', 'sy', 'sx')
- image_loss: float32 [64], P('dp')
- mean_loss: float32 [], replicated
The draws below stay inside these ranges and needn't reach their ends.
All inputs are finite; a program needn't handle non-finite values.
Results may differ from the reference program's by a relative error of at most 0.012.
Values may be sent and summed in bfloat16 or wider, within the bound.
No kernel may reach another device: no remote copies, remote signals or barrier semaphores. Data moves between devices by JAX's collectives and lax.ppermute only.
A program may use at most 64 MiB of HBM per device.

```python
import jax
import jax.numpy as jnp
from jax import lax

FEAT = 256
MID = 64
CLASSES = 1000
BLOCKS = 3
GRID = 50
IMAGES = 64
SIDE_H = 56
SIDE_W = 56


def draw_features(key, part):
    key_mean = jax.random.fold_in(key, 11)
    key_noise = jax.random.fold_in(key, 12)
    key_level = jax.random.fold_in(key, 14)
    key_spread = jax.random.fold_in(key, 15)
    key_amount = jax.random.fold_in(key, 16)
    key_tilt = jax.random.fold_in(key, 17)
    row_index = jnp.arange(SIDE_H, dtype=jnp.int32)
    col_index = jnp.arange(SIDE_W, dtype=jnp.int32)
    upper = jnp.where(row_index < SIDE_H // 2, 1.0, -1.0).astype(jnp.float32)
    leftside = jnp.where(col_index < SIDE_W // 2, 1.0, -1.0).astype(jnp.float32)
    quadrant = upper[:, None] * leftside[None, :]
    level = jax.random.uniform(key_level, (IMAGES,), jnp.float32, 0.5, 2.0)
    spread = jax.random.uniform(key_spread, (IMAGES,), jnp.float32, 0.35, 1.75)
    amount = jax.random.uniform(key_amount, (IMAGES,), jnp.float32, 0.5, 1.1)
    pattern = jax.random.normal(key_mean, (FEAT,), jnp.float32)
    tilt = jax.random.normal(key_tilt, (FEAT,), jnp.float32)
    noise = jax.random.normal(key_noise, (IMAGES, SIDE_H, SIDE_W, FEAT), jnp.float32)
    value = level[:, None, None, None] * pattern[None, None, None, :]
    value = value + 0.8 * amount[:, None, None, None] * quadrant[None, :, :, None] * tilt[None, None, None, :]
    value = value + spread[:, None, None, None] * noise
    return jnp.clip(value, -8.0, 8.0).astype(jnp.bfloat16)


def plant(result, key, low, largest):
    index_at = [jax.random.randint(jax.random.fold_in(key, axis), (), 0, length) for axis, length in enumerate(result.shape)]
    main_axis = result.shape.index(max(result.shape))
    neighbour = index_at[:main_axis] + [(index_at[main_axis] + 1) % result.shape[main_axis]] + index_at[main_axis + 1:]
    return result.at[tuple(index_at)].set(low).at[tuple(neighbour)].set(largest)


def shard_levels(stream_key, dims, pieces, low, largest):
    level = 1.0
    for axis_at, shards_of in pieces:
        draws = jax.random.uniform(jax.random.fold_in(jax.random.fold_in(stream_key, 6), axis_at), (shards_of,), jnp.float32, low / len(pieces), largest / len(pieces))
        level = level * jnp.repeat(jnp.exp(draws), dims[axis_at] // shards_of).reshape((-1,) + (1,) * (len(dims) - 1 - axis_at))
    return level


def normal_values(key, extent, scale, reach, shards=(), kind=jnp.bfloat16):
    loudness = shard_levels(key, extent, shards, -0.22, 0.18) if shards else 1.0
    array = jax.random.normal(key, extent, jnp.float32) * scale * loudness
    return jnp.minimum(jnp.maximum(array, -reach), reach).astype(kind)


def setup_inputs(seed: int = 0) -> dict:
    splits = jax.random.split(jax.random.key(seed), 16)
    features = draw_features(jax.random.fold_in(splits[15], 71), 0)
    labels = plant(jax.random.randint(splits[1], (IMAGES,), 0, CLASSES), jax.random.fold_in(splits[1], 1), 0, CLASSES - 1).astype(jnp.int32)
    grid = jax.random.randint(splits[2], (2,), 0, GRID).astype(jnp.int32)
    w_reduce = normal_values(splits[3], (BLOCKS, FEAT, MID), FEAT ** -0.5, 0.375, ((2, 64),))
    w_spatial = normal_values(splits[4], (BLOCKS, 3, 3, MID, MID), (9 * MID) ** -0.5, 0.25, ((4, 64),))
    w_expand = normal_values(splits[5], (BLOCKS, MID, FEAT), MID ** -0.5, 0.75, ((2, 64),))
    w_class = normal_values(splits[6], (FEAT, CLASSES), (FEAT // 16) ** -0.5, 1.5, ((0, 64),))
    dir_reduce = normal_values(splits[7], (2, BLOCKS, FEAT, MID), 1.0, 6.0, ((3, 64),))
    dir_spatial = normal_values(splits[8], (2, BLOCKS, 3, 3, MID, MID), 1.0, 6.0, ((5, 64),))
    dir_expand = normal_values(splits[9], (2, BLOCKS, MID, FEAT), 1.0, 6.0, ((3, 64),))
    dir_class = normal_values(splits[10], (2, FEAT, CLASSES), 1.0, 6.0, ((1, 64),))
    gain_mid = jnp.clip(1.0 + 0.1 * jax.random.normal(splits[11], (BLOCKS, 2, MID), jnp.float32), 0.5, 1.5)
    shift_mid = normal_values(splits[12], (BLOCKS, 2, MID), 0.5, 3.0, (), jnp.float32)
    gain_out = jnp.clip(1.0 + 0.1 * jax.random.normal(splits[13], (BLOCKS, FEAT), jnp.float32), 0.5, 1.5)
    shift_out = normal_values(splits[14], (BLOCKS, FEAT), 0.5, 3.0, (), jnp.float32)
    return {"features": features, "labels": labels, "grid": grid, "w_reduce": w_reduce, "w_spatial": w_spatial, "w_expand": w_expand, "w_class": w_class, "dir_reduce": dir_reduce, "dir_spatial": dir_spatial, "dir_expand": dir_expand, "dir_class": dir_class, "gain_mid": gain_mid, "shift_mid": shift_mid, "gain_out": gain_out, "shift_out": shift_out}


EPS_NORM = 1e-06
EPS_BN = 1e-05

def coefficients(grid):
    values = grid.astype(jnp.float32)
    alpha = (2.0 * values + 1.0 - GRID) / GRID
    return (alpha[0], alpha[1])

def filter_ratio(base, direction, axes):
    base_norm = jnp.sqrt(lax.optimization_barrier(jnp.sum(jnp.square(base.astype(jnp.float32)), axis=axes, keepdims=True)))
    dir_norm = jnp.sqrt(lax.optimization_barrier(jnp.sum(jnp.square(direction.astype(jnp.float32)), axis=axes, keepdims=True)) + EPS_NORM)
    return base_norm / dir_norm

def perturb(base, dir_a, dir_b, axes, alpha_a, alpha_b):
    ratio_a = filter_ratio(base, dir_a, axes)
    ratio_b = filter_ratio(base, dir_b, axes)
    value = base.astype(jnp.float32) + alpha_a * ratio_a * dir_a.astype(jnp.float32) + alpha_b * ratio_b * dir_b.astype(jnp.float32)
    return value.astype(jnp.bfloat16)

def batch_norm(y, gain, shift):
    axes = (0, 1, 2)
    mean = lax.optimization_barrier(jnp.mean(y, axis=axes))
    centred = y - mean
    var = lax.optimization_barrier(jnp.mean(centred * centred, axis=axes))
    return centred * lax.rsqrt(var + EPS_BN) * gain + shift

def pointwise(x, weight):
    shape = x.shape
    flat = jnp.dot(x.reshape(-1, shape[-1]), weight, preferred_element_type=jnp.float32)
    return flat.reshape(shape[:-1] + (weight.shape[-1],))

def reference(features, labels, grid, w_reduce, w_spatial, w_expand, w_class, dir_reduce, dir_spatial, dir_expand, dir_class, gain_mid, shift_mid, gain_out, shift_out):
    alpha_a, alpha_b = coefficients(grid)
    current = features
    for block in range(BLOCKS):
        p_reduce = perturb(w_reduce[block], dir_reduce[0, block], dir_reduce[1, block], (0,), alpha_a, alpha_b)
        p_spatial = perturb(w_spatial[block], dir_spatial[0, block], dir_spatial[1, block], (0, 1, 2), alpha_a, alpha_b)
        p_expand = perturb(w_expand[block], dir_expand[0, block], dir_expand[1, block], (0,), alpha_a, alpha_b)
        first = pointwise(current, p_reduce)
        first = jax.nn.relu(batch_norm(first, gain_mid[block, 0], shift_mid[block, 0])).astype(jnp.bfloat16)
        second = lax.conv_general_dilated(first, p_spatial, (1, 1), 'SAME', dimension_numbers=('NHWC', 'HWIO', 'NHWC'), preferred_element_type=jnp.float32)
        second = jax.nn.relu(batch_norm(second, gain_mid[block, 1], shift_mid[block, 1])).astype(jnp.bfloat16)
        third = batch_norm(pointwise(second, p_expand), gain_out[block], shift_out[block])
        current = jax.nn.relu(current.astype(jnp.float32) + third).astype(jnp.bfloat16)
    pooled = (lax.optimization_barrier(jnp.sum(current.astype(jnp.float32), axis=(1, 2))) / (SIDE_H * SIDE_W)).astype(jnp.bfloat16)
    p_class = perturb(w_class, dir_class[0], dir_class[1], (0,), alpha_a, alpha_b)
    logits = jnp.dot(pooled, p_class, preferred_element_type=jnp.float32)
    total = jnp.log(lax.optimization_barrier(jnp.sum(jnp.exp(logits), axis=1)))
    classes = lax.broadcasted_iota(jnp.int32, logits.shape, 1)
    picked = lax.optimization_barrier(jnp.sum(jnp.where(classes == labels[:, None], logits, 0.0), axis=1))
    image_loss = total - picked
    mean_loss = jnp.sum(image_loss) / IMAGES
    return (current, image_loss, mean_loss)
```

```python
import functools

import jax
import jax.numpy as jnp
from jax import lax
from jax.experimental import pallas as pl
from jax.experimental.pallas import tpu as pltpu
from jax.sharding import Mesh
from jax.sharding import PartitionSpec as P

BLOCKS = 3
GRID = 50
EPS_NORM = 1e-06
EPS_BN = 1e-05
FEAT = 256
MID = 64
CLASSES = 1000
TILE = 28
OWN = TILE * TILE
SIDE = 32
CELLS = SIDE * SIDE
OWN_ROWS = TILE * SIDE
HALO = SIDE - TILE
DP = ("z", "y", "xh")
ALL = ("z", "y", "xh", "sy", "sx")
TILES = 4
IMAGES = 64

PARAMS = pltpu.CompilerParams(vmem_limit_bytes=32 * 1024 * 1024)
VM = pl.BlockSpec(memory_space=pltpu.VMEM)
SM = pl.BlockSpec(memory_space=pltpu.SMEM)


def own_cells(channels):
    cell = lax.broadcasted_iota(jnp.int32, (OWN_ROWS, channels), 0)
    return (cell & (SIDE - 1)) < TILE


def moments(y):
    own = own_cells(y.shape[1])
    top = y[:OWN_ROWS]
    mean = jnp.sum(jnp.where(own, top, 0.0), axis=0, keepdims=True) * (1.0 / OWN)
    off = jnp.where(own, top - mean, 0.0)
    return jnp.concatenate([mean, jnp.sum(off * off, axis=0, keepdims=True)], axis=1)


def merged(parts, cells):
    count, width = parts.shape[0], parts.shape[1] // 2
    means = parts[:, :width]
    mean = jnp.sum(means, axis=0, keepdims=True) * (1.0 / count)
    off = means - mean
    squares = jnp.sum(parts[:, width:] + cells * (off * off), axis=0, keepdims=True)
    return mean, squares


def normalizer(parts, gain, shift, cells):
    mean, squares = merged(parts, cells)
    scale = lax.rsqrt(squares * (1.0 / (cells * parts.shape[0])) + EPS_BN) * gain
    return lambda y: (y - mean) * scale + shift


def dot_t(left, right):
    return lax.dot_general(
        left, right, (((1,), (1,)), ((), ())), preferred_element_type=jnp.float32
    )


def emit(y, y_ref, out_ref):
    y_ref[...] = y
    out_ref[...] = jnp.broadcast_to(moments(y), out_ref.shape)


def reduce_kernel(x_ref, w_ref, y_ref, out_ref):
    emit(dot_t(x_ref[...], w_ref[...]), y_ref, out_ref)


def spatial_kernel(cells, at_ref, parts_ref, y_ref, gain_ref, shift_ref, w_ref, y2_ref, out_ref, frame):
    norm = normalizer(parts_ref[...], gain_ref[...], shift_ref[...], cells)
    a = jnp.maximum(norm(y_ref[...]), 0.0)
    sy, sx = at_ref[0], at_ref[1]
    cell = lax.broadcasted_iota(jnp.int32, (CELLS, MID), 0)
    col = cell & (SIDE - 1)
    row = ((cell + jnp.where((sx == 1) & (col > TILE), SIDE, 0)) >> 5) & (SIDE - 1)
    inside = (row != SIDE - 1 - 3 * sy) & (col != SIDE - 1 - 3 * sx)
    a = jnp.where(inside, a, 0.0)
    both = jnp.concatenate(
        [pltpu.roll(a, 1, 0), a, pltpu.roll(a, CELLS - 1, 0)], axis=1
    ).astype(jnp.bfloat16)
    frame[SIDE : SIDE + CELLS, :] = both
    frame[0:SIDE, :] = both[CELLS - SIDE :]
    frame[SIDE + CELLS :, :] = both[:SIDE]
    total = None
    for i in range(3):
        term = dot_t(frame[SIDE * i : SIDE * i + CELLS, :], w_ref[:, 3 * MID * i : 3 * MID * (i + 1)])
        total = term if total is None else total + term
    emit(total, y2_ref, out_ref)


def expand_kernel(cells, parts_ref, y_ref, gain_ref, shift_ref, w_ref, y3_ref, out_ref):
    norm = normalizer(parts_ref[...], gain_ref[...], shift_ref[...], cells)
    c = jnp.maximum(norm(y_ref[...]), 0.0).astype(jnp.bfloat16)
    emit(dot_t(c, w_ref[...]), y3_ref, out_ref)


def block_kernel(cells, parts_ref, y_ref, gain_ref, shift_ref, x_ref, w_ref, new_ref, y1_ref, out_ref):
    norm = normalizer(parts_ref[...], gain_ref[...], shift_ref[...], cells)
    new = jnp.maximum(x_ref[...].astype(jnp.float32) + norm(y_ref[...]), 0.0).astype(jnp.bfloat16)
    new_ref[...] = new
    emit(dot_t(new, w_ref[...]), y1_ref, out_ref)


def last_kernel(cells, parts_ref, y_ref, gain_ref, shift_ref, x_ref, new_ref, out_ref):
    norm = normalizer(parts_ref[...], gain_ref[...], shift_ref[...], cells)
    top = x_ref[:OWN_ROWS, :].astype(jnp.float32) + norm(y_ref[:OWN_ROWS, :])
    new = jnp.maximum(top, 0.0).astype(jnp.bfloat16)
    for row in range(TILE):
        new_ref[row] = new[SIDE * row : SIDE * row + TILE]
    kept = jnp.where(own_cells(FEAT), new.astype(jnp.float32), 0.0)
    out_ref[...] = jnp.broadcast_to(jnp.sum(kept, axis=0, keepdims=True), out_ref.shape)


def call(kernel, outs, *args, scratch=(), smem=0):
    return pl.pallas_call(
        kernel,
        out_shape=[jax.ShapeDtypeStruct(s, d) for s, d in outs],
        in_specs=[SM] * smem + [VM] * (len(args) - smem),
        out_specs=[VM] * len(outs),
        scratch_shapes=list(scratch),
        compiler_params=PARAMS,
    )(*args)


def tile_frame(features, sy, sx):
    own = features[0]
    cols = jnp.where(sx == 0, own[:, TILE - HALO :], own[:, :HALO])
    rows = jnp.where(sy == 0, own[TILE - HALO :], own[:HALO])
    corner = jnp.where(sx == 0, rows[:, TILE - HALO :], rows[:, :HALO])
    cols = lax.ppermute(cols, "sx", [(0, 1), (1, 0)])
    rows = lax.ppermute(rows, "sy", [(0, 1), (1, 0)])
    corner = lax.ppermute(corner, ("sy", "sx"), [(i, 3 - i) for i in range(4)])
    right = jnp.concatenate([cols, corner], axis=0)
    right = jnp.where(sx == 1, jnp.concatenate([right[1:], right[:1]], axis=0), right)
    left = jnp.concatenate([own, rows], axis=0)
    return jnp.concatenate([left, right], axis=1).reshape(CELLS, FEAT)


def norm_ratio(base, direction, axis):
    square = lambda v: jnp.sum(v * v, axis=axis, keepdims=True)
    return jnp.sqrt(square(base)) / jnp.sqrt(square(direction) + EPS_NORM)


def perturbed(base, dir_a, dir_b, alpha, axis):
    base, dir_a, dir_b = (v.astype(jnp.float32) for v in (base, dir_a, dir_b))
    value = (
        base
        + alpha[0] * norm_ratio(base, dir_a, axis) * dir_a
        + alpha[1] * norm_ratio(base, dir_b, axis) * dir_b
    )
    return value.astype(jnp.bfloat16)


def spread(row, axes):
    count, width = lax.axis_size(axes), row.size
    pieces = jnp.broadcast_to(row.reshape(1, -1, 128), (count, width // 128, 128))
    return lax.all_to_all(pieces, axes, 0, 0, tiled=True).reshape(count, width)


def per_device(
    features,
    labels,
    grid,
    w_reduce,
    w_spatial,
    w_expand,
    w_class,
    dir_reduce,
    dir_spatial,
    dir_expand,
    dir_class,
    gain_mid,
    shift_mid,
    gain_out,
    shift_out,
):
    sy, sx = lax.axis_index("sy"), lax.axis_index("sx")
    at = jnp.stack([sy, sx]).astype(jnp.int32)
    alpha = (2.0 * grid.astype(jnp.float32) + 1.0 - GRID) / GRID

    with jax.named_scope("filters"):
        p_reduce = perturbed(
            w_reduce[:, :, 0], dir_reduce[0, :, :, 0], dir_reduce[1, :, :, 0], alpha, 1
        )
        first = spread(p_reduce[0], DP)
        p_spatial = perturbed(
            w_spatial[..., 0], dir_spatial[0, ..., 0], dir_spatial[1, ..., 0], alpha, (1, 2, 3)
        ).reshape(BLOCKS, -1)
        p_expand = perturbed(w_expand, dir_expand[0], dir_expand[1], alpha, 1)
        p_expand = jnp.swapaxes(p_expand, 1, 2).reshape(BLOCKS, -1)
        rest = jnp.concatenate([p_reduce[1:].ravel(), p_spatial.ravel(), p_expand.ravel()])
        rest = jnp.pad(rest, (0, -rest.size % 128))

    with jax.named_scope("halo"):
        x = tile_frame(features, sy, sx)

    with jax.named_scope("filters"):
        (y1, sent) = call(
            reduce_kernel, [((CELLS, MID), jnp.float32), ((1, 2 * MID), jnp.float32)], x, first
        )
        every = spread(rest, DP)
        w_r = [first, every[:, :FEAT], every[:, FEAT : 2 * FEAT]]
        at_s, at_e = 2 * FEAT, 2 * FEAT + BLOCKS * 9 * MID
        w_s = [every[:, at_s + b * 9 * MID : at_s + (b + 1) * 9 * MID] for b in range(BLOCKS)]
        w_e = [
            every[:, at_e + b * 4 * MID : at_e + (b + 1) * 4 * MID].reshape(FEAT, MID)
            for b in range(BLOCKS)
        ]

    with jax.named_scope("class"):
        square = lambda v: jnp.sum(jnp.square(v.astype(jnp.float32)), axis=0)
        norms = jnp.concatenate([square(w_class), square(dir_class[0]), square(dir_class[1])])
        norms = jnp.sum(spread(jnp.pad(norms, (0, 72)), DP), axis=0)[: 3 * CLASSES]
        norms = jnp.sqrt(norms.reshape(3, CLASSES) + jnp.array([0.0, EPS_NORM, EPS_NORM])[:, None])
        p_class = (
            w_class.astype(jnp.float32)
            + alpha[0] * (norms[0] / norms[1]) * dir_class[0].astype(jnp.float32)
            + alpha[1] * (norms[0] / norms[2]) * dir_class[1].astype(jnp.float32)
        ).astype(jnp.bfloat16)
        p_class = spread(jnp.pad(p_class, ((0, 0), (0, 24))), DP).reshape(FEAT, 1024)

    exchange = lambda row: spread(row, ALL)
    row = lambda v: v.reshape(1, -1)
    for b in range(BLOCKS):
        with jax.named_scope(f"block_{b}"):
            y2, sent = call(
                functools.partial(spatial_kernel, OWN),
                [((CELLS, MID), jnp.float32), ((1, 2 * MID), jnp.float32)],
                at, exchange(sent), y1, row(gain_mid[b, 0]), row(shift_mid[b, 0]), w_s[b],
                scratch=[pltpu.VMEM((CELLS + 2 * SIDE, 3 * MID), jnp.bfloat16)], smem=1,
            )
            y3, sent = call(
                functools.partial(expand_kernel, OWN),
                [((CELLS, FEAT), jnp.float32), ((1, 2 * FEAT), jnp.float32)],
                exchange(sent), y2, row(gain_mid[b, 1]), row(shift_mid[b, 1]), w_e[b],
            )
            args = (exchange(sent), y3, row(gain_out[b]), row(shift_out[b]), x)
            if b < BLOCKS - 1:
                x, y1, sent = call(
                    functools.partial(block_kernel, OWN),
                    [((CELLS, FEAT), jnp.bfloat16), ((CELLS, MID), jnp.float32), ((1, 2 * MID), jnp.float32)],
                    *args, w_r[b + 1],
                )
            else:
                section, pooled = call(
                    functools.partial(last_kernel, OWN),
                    [((TILE, TILE, FEAT), jnp.bfloat16), ((1, FEAT), jnp.float32)],
                    *args,
                )
    with jax.named_scope("loss"):
        tag = jnp.broadcast_to(labels.astype(jnp.float32)[None], (1, 128))
        every = spread(jnp.concatenate([pooled, tag, tag], axis=1), ALL).reshape(IMAGES, TILES, -1)
        pooled = (jnp.sum(every[:, :, :FEAT], axis=1) / (OWN * TILES)).astype(jnp.bfloat16)
        tags = every[:, 0, FEAT].astype(jnp.int32)
        logits = jnp.dot(pooled, p_class, preferred_element_type=jnp.float32)[:, :CLASSES]
        summed = jnp.log(jnp.sum(jnp.exp(logits), axis=1))
        classes = lax.broadcasted_iota(jnp.int32, logits.shape, 1)
        picked = jnp.sum(jnp.where(classes == tags[:, None], logits, 0.0), axis=1)
        losses = summed - picked
        mean_loss = jnp.sum(losses) / IMAGES
        image_loss = lax.dynamic_slice(losses, (lax.axis_index(DP),), (1,))
    return section[None], image_loss, mean_loss


def solution(mesh):
    split = Mesh(
        mesh.devices.reshape(8, 4, 2, mesh.shape["sy"], mesh.shape["sx"]), ALL
    )
    tiles = P(DP, "sy", "sx", None)
    return jax.shard_map(
        per_device,
        mesh=split,
        in_specs=(
            tiles,
            P(DP),
            P(),
            P(None, None, DP),
            P(None, None, None, None, DP),
            P(None, None, DP),
            P(DP, None),
            P(None, None, None, DP),
            P(None, None, None, None, None, DP),
            P(None, None, None, DP),
            P(None, DP, None),
            P(),
            P(),
            P(),
            P(),
        ),
        out_specs=(tiles, P(DP), P()),
        check_vma=False,
    )
```

```python
import functools

import jax
import jax.numpy as jnp
import numpy as np
from jax import lax
from jax.experimental import pallas as pl
from jax.experimental.pallas import tpu as pltpu
from jax.sharding import Mesh
from jax.sharding import PartitionSpec as P

BLOCKS = 3
GRID = 50
EPS_NORM = 1e-06
EPS_BN = 1e-05
FEAT = 256
MID = 64
CLASSES = 1000
TILE = 28
OWN = TILE * TILE
SIDE = 32
CELLS = SIDE * SIDE
OWN_ROWS = TILE * SIDE
HALO = SIDE - TILE
DP = ("z4", "z2", "y", "xh")
GROUP = ("z2", "y", "xh", "sy", "sx")
ALL = ("z4",) + GROUP
TILES = 4
HELD = 4
PAIRS = HELD // 2
IMAGES = 64
CLASS_PART = 16

FILTER_OF_ROW = np.concatenate(
    [np.repeat(np.arange(3), 4), np.arange(3, 15), np.repeat(np.arange(15, 18), 9), np.full(5, 18)]
)
ROWS = FILTER_OF_ROW.size
SAME_FILTER = (FILTER_OF_ROW[:, None] == FILTER_OF_ROW[None]).astype(np.float32)

PARAMS = pltpu.CompilerParams(vmem_limit_bytes=40 * 1024 * 1024)
VM = pl.BlockSpec(memory_space=pltpu.VMEM)
SM = pl.BlockSpec(memory_space=pltpu.SMEM)


def dot_t(left, right):
    return lax.dot_general(
        left, right, (((1,), (1,)), ((), ())), preferred_element_type=jnp.float32
    )


def tile_moments(y):
    cells = y[:OWN_ROWS].reshape(TILE, SIDE, y.shape[1])
    mean = jnp.sum(jnp.sum(cells, axis=0)[:TILE], axis=0, keepdims=True) * (1.0 / OWN)
    off = cells - mean[None]
    return mean, jnp.sum(jnp.sum(off * off, axis=0)[:TILE], axis=0, keepdims=True)


def halves(pair):
    return [pair[:, :MID], pair[:, MID:]]


def merged(means, squares, cells):
    mean = functools.reduce(jnp.add, means) * (1.0 / len(means))
    total = functools.reduce(jnp.add, squares)
    for m in means:
        total = total + cells * ((m - mean) * (m - mean))
    return mean, total


def normalizer(parts, gain, shift, cells, pairs=False):
    count, width = parts.shape[0], parts.shape[1] // 2
    means = parts[:, :width]
    mean = jnp.sum(means, axis=0, keepdims=True) * (1.0 / count)
    off = means - mean
    squares = jnp.sum(parts[:, width:] + cells * (off * off), axis=0, keepdims=True)
    scale = lax.rsqrt(squares * (1.0 / (cells * count)) + EPS_BN) * gain
    if pairs:
        mean, scale, shift = (jnp.concatenate([v, v], axis=1) for v in (mean, scale, shift))
    return lambda y: (y - mean) * scale + shift


def send_moments(out_ref, tiles):
    mean, squares = merged([t[0] for t in tiles], [t[1] for t in tiles], OWN)
    out_ref[...] = jnp.concatenate([mean, squares], axis=1)


def pair_moments(pair):
    mean, squares = tile_moments(pair)
    return list(zip(halves(mean), halves(squares)))


def filter_kernel(grid_ref, same_ref, raw_ref, out_ref):
    alpha = [(2.0 * grid_ref[k].astype(jnp.float32) + 1.0 - GRID) / GRID for k in range(2)]

    def norm(k, eps):
        v = raw_ref[k]
        total = jnp.sum(
            jnp.dot(same_ref[...], v * v, precision=lax.Precision.HIGHEST, preferred_element_type=jnp.float32),
            axis=1,
            keepdims=True,
        )
        return jnp.sqrt(total + eps)

    base = norm(0, 0.0)
    value = raw_ref[0]
    for k in range(2):
        value = value + (alpha[k] * (base / norm(k + 1, EPS_NORM))) * raw_ref[k + 1]
    out_ref[...] = value.astype(jnp.bfloat16)


def reduce_kernel(x_ref, w_ref, out_ref):
    send_moments(out_ref, [tile_moments(dot_t(x_ref[...], w_ref[...]))])


def reduced_pair(first, second, w):
    zero = jnp.zeros_like(w)
    return dot_t(first, jnp.concatenate([w, zero], axis=0)) + dot_t(
        second, jnp.concatenate([zero, w], axis=0)
    )


def spatial_kernel(cells, fresh, parts_ref, y_ref, gain_ref, shift_ref, inside_ref, w_ref, *rest):
    reduce_ref = rest[0] if fresh else None
    y2_ref, out_ref, frame = rest[-3:]
    norm = normalizer(parts_ref[...], gain_ref[...], shift_ref[...], cells, True)
    tiles = []
    for p in range(PAIRS):
        if fresh:
            y = reduced_pair(y_ref[2 * p], y_ref[2 * p + 1], reduce_ref[...])
        else:
            y = y_ref[p]
        a = jnp.maximum(norm(y), 0.0) * inside_ref[...]
        for j, v in enumerate((pltpu.roll(a, 1, 0), a, pltpu.roll(a, CELLS - 1, 0))):
            v = v.astype(jnp.bfloat16)
            lanes = slice(2 * MID * j, 2 * MID * (j + 1))
            frame[p, SIDE : SIDE + CELLS, lanes] = v
            frame[p, 0:SIDE, lanes] = v[CELLS - SIDE :]
            frame[p, SIDE + CELLS :, lanes] = v[:SIDE]
        total = None
        for i in range(3):
            term = dot_t(frame[p, SIDE * i : SIDE * i + CELLS, :], w_ref[i])
            total = term if total is None else total + term
        y2_ref[p] = total
        tiles += pair_moments(total)
    send_moments(out_ref, tiles)


def expand_kernel(cells, parts_ref, y_ref, gain_ref, shift_ref, w_ref, c_ref, out_ref):
    norm = normalizer(parts_ref[...], gain_ref[...], shift_ref[...], cells, True)
    tiles = []
    for p in range(PAIRS):
        c = jnp.maximum(norm(y_ref[p]), 0.0).astype(jnp.bfloat16)
        c_ref[p] = c
        for h in range(2):
            tiles.append(tile_moments(dot_t(c[:OWN_ROWS], w_ref[h])))
    send_moments(out_ref, tiles)


def block_kernel(cells, parts_ref, c_ref, gain_ref, shift_ref, x_ref, w_ref, next_ref, new_ref, y1_ref, out_ref):
    norm = normalizer(parts_ref[...], gain_ref[...], shift_ref[...], cells)
    tiles = []
    for p in range(PAIRS):
        pair = []
        for h in range(2):
            y = dot_t(c_ref[p], w_ref[h])
            new = jnp.maximum(x_ref[2 * p + h].astype(jnp.float32) + norm(y), 0.0).astype(jnp.bfloat16)
            new_ref[2 * p + h] = new
            pair.append(new)
        y1 = reduced_pair(*pair, next_ref[...])
        y1_ref[p] = y1
        tiles += pair_moments(y1)
    send_moments(out_ref, tiles)


def last_kernel(cells, at_ref, parts_ref, c_ref, gain_ref, shift_ref, x_ref, w_ref, new_ref, out_ref):
    norm = normalizer(parts_ref[...], gain_ref[...], shift_ref[...], cells)
    for k in range(HELD):
        y = dot_t(c_ref[k // 2, :OWN_ROWS, :], w_ref[k % 2])
        top = x_ref[k, :OWN_ROWS, :].astype(jnp.float32) + norm(y)
        new = jnp.maximum(top, 0.0).astype(jnp.bfloat16)

        @pl.when(at_ref[0] == k)
        def _():
            for row in range(TILE):
                new_ref[row] = new[SIDE * row : SIDE * row + TILE]

        by_col = jnp.sum(new.astype(jnp.float32).reshape(TILE, SIDE, FEAT), axis=0)
        out_ref[k : k + 1, :] = jnp.sum(by_col[:TILE], axis=0, keepdims=True)


def call(kernel, outs, *args, scratch=(), smem=0):
    return pl.pallas_call(
        kernel,
        out_shape=[jax.ShapeDtypeStruct(s, d) for s, d in outs],
        in_specs=[SM] * smem + [VM] * (len(args) - smem),
        out_specs=[VM] * len(outs),
        scratch_shapes=list(scratch),
        compiler_params=PARAMS,
    )(*args)


def tile_frame(features, sy, sx):
    own = features[0]
    cols = jnp.where(sx == 0, own[:, TILE - HALO :], own[:, :HALO])
    rows = jnp.where(sy == 0, own[TILE - HALO :], own[:HALO])
    corner = jnp.where(sx == 0, rows[:, TILE - HALO :], rows[:, :HALO])
    cols = lax.ppermute(cols, "sx", [(0, 1), (1, 0)])
    rows = lax.ppermute(rows, "sy", [(0, 1), (1, 0)])
    corner = lax.ppermute(corner, ("sy", "sx"), [(i, 3 - i) for i in range(4)])
    right = jnp.concatenate([cols, corner], axis=0)
    right = jnp.where(sx == 1, jnp.concatenate([right[1:], right[:1]], axis=0), right)
    left = jnp.concatenate([own, rows], axis=0)
    return jnp.concatenate([left, right], axis=1).reshape(CELLS, FEAT)


def inside_image(sy, sx):
    cell = lax.broadcasted_iota(jnp.int32, (CELLS, 2 * MID), 0)
    col = cell % SIDE
    row = ((cell + jnp.where((sx == 1) & (col > TILE), SIDE, 0)) // SIDE) % SIDE
    inside = (row != SIDE - 1 - 3 * sy) & (col != SIDE - 1 - 3 * sx)
    return inside.astype(jnp.float32)


def spread(row, axes):
    count, width = lax.axis_size(axes), row.size
    pieces = jnp.broadcast_to(row.reshape(1, -1, 128), (count, width // 128, 128))
    return lax.all_to_all(pieces, axes, 0, 0, tiled=True).reshape(count, width)


def held_tiles(own, z4):
    fore, back = [(i, (i + 1) % 4) for i in range(4)], [((i + 1) % 4, i) for i in range(4)]
    below = lax.ppermute(own, "z4", fore)
    above = lax.ppermute(own, "z4", back)

    def finish(after):
        below_, above_, after_ = lax.optimization_barrier((below, above, after))
        half = CELLS // 2
        far = jnp.concatenate(
            [lax.ppermute(below_[:half], "z4", fore), lax.ppermute(above_[half:], "z4", back)], axis=0
        )
        held = jnp.zeros((HELD, CELLS, FEAT), jnp.bfloat16)
        for off, tile in ((0, own), (1, above_), (2, far), (3, below_)):
            held = lax.dynamic_update_slice(held, tile[None], ((z4 + off) % 4, 0, 0))
        return held, after_

    return finish


def paired_spatial(w):
    w = w.reshape(MID, 3, 3, MID)
    zero = jnp.zeros_like(w)
    top, bottom = jnp.concatenate([w, zero], axis=3), jnp.concatenate([zero, w], axis=3)
    both = jnp.concatenate([top, bottom], axis=0)
    return jnp.moveaxis(both, 1, 0).reshape(3, 2 * MID, 3 * 2 * MID)


def paired_expand(w):
    return jnp.stack([jnp.pad(w, ((0, 0), (0, MID))), jnp.pad(w, ((0, 0), (MID, 0)))])


def per_device(
    features,
    labels,
    grid,
    w_reduce,
    w_spatial,
    w_expand,
    w_class,
    dir_reduce,
    dir_spatial,
    dir_expand,
    dir_class,
    gain_mid,
    shift_mid,
    gain_out,
    shift_out,
):
    z4, sy, sx = (lax.axis_index(a) for a in ("z4", "sy", "sx"))
    tile = 2 * sy + sx
    alpha = (2.0 * grid.astype(jnp.float32) + 1.0 - GRID) / GRID

    with jax.named_scope("halo"):
        own = tile_frame(features, sy, sx)
        finish = held_tiles(own, z4)
        inside = inside_image(sy, sx)

    with jax.named_scope("filters"):
        def rows_of(reduce, spatial, expand):
            return jnp.concatenate(
                [
                    reduce[:, :, 0].reshape(12, MID),
                    jnp.swapaxes(expand, 1, 2).reshape(12, MID),
                    spatial[..., 0].reshape(27, MID),
                    jnp.zeros((ROWS - 51, MID), jnp.bfloat16),
                ],
                axis=0,
            )

        raw = jnp.stack(
            [rows_of(w_reduce, w_spatial, w_expand)]
            + [rows_of(dir_reduce[k], dir_spatial[k], dir_expand[k]) for k in range(2)]
        ).astype(jnp.float32)
        (mine,) = call(
            filter_kernel, [((ROWS, MID), jnp.bfloat16)], grid, jnp.asarray(SAME_FILTER), raw, smem=1
        )
        mine = lax.dynamic_slice(mine.reshape(TILES, 7, 128), (tile, 0, 0), (1, 7, 128))
        mine = jnp.broadcast_to(mine, (256, 7, 128))
        pick = lambda v: lax.dynamic_slice(v, (tile, 0), (1, CLASSES))
        rows = jnp.concatenate([pick(w_class), pick(dir_class[0]), pick(dir_class[1])], axis=0)
        rows = jnp.pad(rows, ((0, 0), (0, 64 * CLASS_PART - CLASSES))).reshape(3, 64, CLASS_PART)
        rows = jnp.moveaxis(rows, 0, 1).reshape(64, 3 * CLASS_PART)
        tag = jnp.concatenate([labels // 32, labels % 32]).astype(jnp.bfloat16)
        rows = jnp.concatenate(
            [rows, jnp.broadcast_to(tag, (64, 2)), jnp.zeros((64, 126 - 3 * CLASS_PART), jnp.bfloat16)], axis=1
        )
        rows = jnp.broadcast_to(rows[None], (4, 64, 128)).reshape(256, 1, 128)
        every = lax.all_to_all(jnp.concatenate([mine, rows], axis=1), ALL, 0, 0, tiled=True)
        rows = every[:, 7, :]
        every = every[:, :7, :].reshape(64, 2 * ROWS // 4 * 128)
        w_r = [every[:, FEAT * b : FEAT * (b + 1)] for b in range(BLOCKS)]
        w_e, w_s = [], []
        for b in range(BLOCKS):
            at = FEAT * (BLOCKS + b)
            w_e.append(paired_expand(every[:, at : at + FEAT].reshape(FEAT, MID)))
            at = FEAT * 2 * BLOCKS + 9 * MID * b
            w_s.append(paired_spatial(every[:, at : at + 9 * MID]))

    w_first, = w_r[:1]
    held, w_first = finish(w_first)
    (sent,) = call(reduce_kernel, [((1, 2 * MID), jnp.float32)], own, w_first)

    with jax.named_scope("class"):
        high, low = (rows[::TILES, 3 * CLASS_PART + k].astype(jnp.int32) for k in range(2))
        table = high * 32 + low
        tags = table.reshape(4, 16).T.reshape(IMAGES)
        raw = rows[:, : 3 * CLASS_PART].astype(jnp.float32).reshape(FEAT, 3, CLASS_PART)
        norms = jnp.sum(raw * raw, axis=0)
        base = jnp.sqrt(norms[0])
        p_class = raw[:, 0]
        for k in range(2):
            p_class = p_class + alpha[k] * (base / jnp.sqrt(norms[k + 1] + EPS_NORM)) * raw[:, k + 1]
        p_class = p_class.astype(jnp.bfloat16)

    row = lambda v: v.reshape(1, -1)
    cells = OWN
    axes = ALL
    y1 = held
    x = held
    for b in range(BLOCKS):
        with jax.named_scope(f"block_{b}"):
            fresh = b == 0
            y2, sent = call(
                functools.partial(spatial_kernel, cells, fresh),
                [((PAIRS, CELLS, 2 * MID), jnp.float32), ((1, 2 * MID), jnp.float32)],
                spread(sent, axes), y1, row(gain_mid[b, 0]), row(shift_mid[b, 0]), inside, w_s[b],
                *([w_first] if fresh else []),
                scratch=[pltpu.VMEM((PAIRS, CELLS + 2 * SIDE, 6 * MID), jnp.bfloat16)],
            )
            cells, axes = HELD * OWN, GROUP
            c, sent = call(
                functools.partial(expand_kernel, cells),
                [((PAIRS, CELLS, 2 * MID), jnp.bfloat16), ((1, 2 * FEAT), jnp.float32)],
                spread(sent, axes), y2, row(gain_mid[b, 1]), row(shift_mid[b, 1]), w_e[b],
            )
            args = (spread(sent, axes), c, row(gain_out[b]), row(shift_out[b]), x, w_e[b])
            if b < BLOCKS - 1:
                x, y1, sent = call(
                    functools.partial(block_kernel, cells),
                    [
                        ((HELD, CELLS, FEAT), jnp.bfloat16),
                        ((PAIRS, CELLS, 2 * MID), jnp.float32),
                        ((1, 2 * MID), jnp.float32),
                    ],
                    *args, w_r[b + 1],
                )
            else:
                section, pooled = call(
                    functools.partial(last_kernel, cells),
                    [((TILE, TILE, FEAT), jnp.bfloat16), ((HELD, FEAT), jnp.float32)],
                    z4.astype(jnp.int32).reshape(1), *args, smem=1,
                )
    with jax.named_scope("loss"):
        every = spread(pooled, GROUP).reshape(16, TILES, HELD, FEAT)
        pooled = (jnp.sum(every, axis=1) / (OWN * TILES)).astype(jnp.bfloat16).reshape(IMAGES, FEAT)
        logits = jnp.dot(pooled, p_class, preferred_element_type=jnp.float32)
        classes = lax.broadcasted_iota(jnp.int32, logits.shape, 1) + CLASS_PART * lax.axis_index(GROUP)
        terms = jnp.sum(jnp.where(classes < CLASSES, jnp.exp(logits), 0.0), axis=1)
        picked = jnp.sum(jnp.where(classes == tags[:, None], logits, 0.0), axis=1)
        total = jnp.sum(spread(jnp.concatenate([terms, picked]), GROUP), axis=0)
        losses = jnp.log(total[:IMAGES]) - total[IMAGES:]
        mean_loss = jnp.sum(losses) / IMAGES
        mine = HELD * lax.axis_index(("z2", "y", "xh")) + z4
        image_loss = lax.dynamic_slice(losses, (mine,), (1,))
    return section[None], image_loss, mean_loss


def solution(mesh):
    split = Mesh(
        mesh.devices.reshape(4, 2, 4, 2, mesh.shape["sy"], mesh.shape["sx"]), ALL
    )
    tiles = P(DP, "sy", "sx", None)
    return jax.shard_map(
        per_device,
        mesh=split,
        in_specs=(
            tiles,
            P(DP),
            P(),
            P(None, None, DP),
            P(None, None, None, None, DP),
            P(None, None, DP),
            P(DP, None),
            P(None, None, None, DP),
            P(None, None, None, None, None, DP),
            P(None, None, None, DP),
            P(None, DP, None),
            P(),
            P(),
            P(),
            P(),
        ),
        out_specs=(tiles, P(DP), P()),
        check_vma=False,
    )
```

```python
import functools

import jax
import jax.numpy as jnp
from jax import lax
from jax.experimental import pallas as pl
from jax.experimental.pallas import tpu as pltpu
from jax.sharding import Mesh
from jax.sharding import PartitionSpec as P

BLOCKS = 3
GRID = 50
EPS_NORM = 1e-06
EPS_BN = 1e-05
FEAT = 256
MID = 64
CLASSES = 1000
TILE = 28
OWN = TILE * TILE
SIDE = 32
CELLS = SIDE * SIDE
OWN_ROWS = TILE * SIDE
HALO = SIDE - TILE
DP = ("z4", "z2", "y", "xh")
GROUP = ("z2", "y", "xh", "sy", "sx")
ALL = ("z4",) + GROUP
TILES = 4
HELD = 4
PAIRS = HELD // 2
IMAGES = 64
CLASS_PART = 16

ROWS = 56
FLAT = 40

PARAMS = pltpu.CompilerParams(vmem_limit_bytes=16 * 1024 * 1024)
VM = pl.BlockSpec(memory_space=pltpu.VMEM)
SM = pl.BlockSpec(memory_space=pltpu.SMEM)


def dot_t(left, right):
    return lax.dot_general(
        left, right, (((1,), (1,)), ((), ())), preferred_element_type=jnp.float32
    )


def tile_moments(y):
    cells = y[:OWN_ROWS].reshape(TILE, SIDE, y.shape[1])
    mean = jnp.sum(jnp.sum(cells, axis=0)[:TILE], axis=0, keepdims=True) * (1.0 / OWN)
    off = cells - mean[None]
    return mean, jnp.sum(jnp.sum(off * off, axis=0)[:TILE], axis=0, keepdims=True)


def halves(pair):
    return [pair[:, :MID], pair[:, MID:]]


def merged(means, squares, cells):
    mean = functools.reduce(jnp.add, means) * (1.0 / len(means))
    total = functools.reduce(jnp.add, squares)
    for m in means:
        total = total + cells * ((m - mean) * (m - mean))
    return mean, total


def normalizer(parts, gain, shift, cells, pairs=False):
    count = parts.shape[0]
    split = (lambda v: (v[:, :2], v[:, 2:])) if parts.ndim == 3 else (lambda v: (v[:, :MID], v[:, MID:]))
    means, squares = split(parts)
    mean = jnp.sum(means, axis=0, keepdims=True) * (1.0 / count)
    off = means - mean
    var = jnp.sum(squares + cells * (off * off), axis=0, keepdims=True) * (1.0 / (cells * count))
    if parts.ndim == 3:
        mean, var = (jnp.concatenate([v[0, :1], v[0, 1:]], axis=1) for v in (mean, var))
    scale = lax.rsqrt(var + EPS_BN) * gain
    if pairs:
        mean, scale, shift = (jnp.concatenate([v, v], axis=1) for v in (mean, scale, shift))
    return lambda y: (y - mean) * scale + shift


def send(out_ref, row):
    for k in range(out_ref.shape[1]):
        piece = row[:, 128 * k : 128 * (k + 1)].reshape(1, 1, 128)
        out_ref[:, k : k + 1, :] = jnp.broadcast_to(piece, (out_ref.shape[0], 1, 128))


def send_moments(out_ref, tiles):
    mean, squares = merged([t[0] for t in tiles], [t[1] for t in tiles], OWN)
    send(out_ref, jnp.concatenate([mean, squares], axis=1))


def pair_moments(pair):
    mean, squares = tile_moments(pair)
    return list(zip(halves(mean), halves(squares)))


def filter_of(index):
    spatial = jnp.where(index < 21, 3, jnp.where(index < 30, 4, jnp.where(index < 39, 5, 18)))
    return jnp.where(index < 12, index >> 2, jnp.where(index < FLAT, spatial, index))


def filter_kernel(grid_ref, raw_ref, out_ref):
    down = filter_of(lax.broadcasted_iota(jnp.int32, (ROWS, ROWS), 0))
    same = (down == filter_of(lax.broadcasted_iota(jnp.int32, (ROWS, ROWS), 1))).astype(jnp.float32)
    alpha = [(2.0 * grid_ref[k].astype(jnp.float32) + 1.0 - GRID) / GRID for k in range(2)]

    def norm(k, eps):
        v = raw_ref[k]
        total = jnp.sum(
            jnp.dot(same, v * v, precision=lax.Precision.HIGHEST, preferred_element_type=jnp.float32),
            axis=1,
            keepdims=True,
        )
        return jnp.sqrt(total + eps)

    base = norm(0, 0.0)
    value = raw_ref[0]
    for k in range(2):
        value = value + (alpha[k] * (base / norm(k + 1, EPS_NORM))) * raw_ref[k + 1]
    out_ref[...] = value.astype(jnp.bfloat16)


def reduce_kernel(x_ref, w_ref, out_ref):
    send_moments(out_ref, [tile_moments(dot_t(x_ref[...], w_ref[...]))])


def reduced_pair(first, second, w):
    zero = jnp.zeros_like(w)
    return dot_t(first, jnp.concatenate([w, zero], axis=0)) + dot_t(
        second, jnp.concatenate([zero, w], axis=0)
    )


def tile_at(k):
    return slice(CELLS * k, CELLS * (k + 1))


def reduce_of(flat_ref, block):
    return flat_ref[:, FEAT * block : FEAT * (block + 1)]


def spatial_of(flat_ref, block):
    start = FEAT * BLOCKS + 9 * MID * block
    taps = [flat_ref[:, start + MID * t : start + MID * (t + 1)] for t in range(9)]
    zero = jnp.zeros_like(taps[0])
    rows = []
    for i in range(3):
        first = [v for t in taps[3 * i : 3 * i + 3] for v in (t, zero)]
        second = [v for t in taps[3 * i : 3 * i + 3] for v in (zero, t)]
        rows.append(jnp.concatenate([jnp.concatenate(v, axis=1) for v in (first, second)], axis=0))
    return rows


def expand_of(expand_ref, block):
    w = expand_ref[:, MID * block : MID * (block + 1)]
    zero = jnp.zeros_like(w)
    return [jnp.concatenate(v, axis=1) for v in ((w, zero), (zero, w))]


def convolved(y, norm, inside, taps, frame):
    a = jnp.maximum(norm(y), 0.0) * inside
    for j, v in enumerate((pltpu.roll(a, 1, 0), a, pltpu.roll(a, CELLS - 1, 0))):
        v = v.astype(jnp.bfloat16)
        lanes = slice(2 * MID * j, 2 * MID * (j + 1))
        frame[SIDE : SIDE + CELLS, lanes] = v
        frame[0:SIDE, lanes] = v[CELLS - SIDE :]
        frame[SIDE + CELLS :, lanes] = v[:SIDE]
    total = None
    for i in range(3):
        term = dot_t(frame[SIDE * i : SIDE * i + CELLS, :], taps[i])
        total = term if total is None else total + term
    return total


def first_own_kernel(parts_ref, x_ref, gain_ref, shift_ref, inside_ref, flat_ref, out_ref, frame):
    norm = normalizer(parts_ref[...], gain_ref[...], shift_ref[...], OWN, True)
    y = reduced_pair(x_ref[...], x_ref[...], reduce_of(flat_ref, 0))
    y2 = convolved(y, norm, inside_ref[...], spatial_of(flat_ref, 0), frame.at[0])
    send_moments(out_ref, pair_moments(y2)[:1])


def expanded(c, pair_weights, tiles):
    for w in pair_weights:
        tiles.append(tile_moments(dot_t(c[:OWN_ROWS], w)))


def first_expand_kernel(
    at_ref, parts_ref, parts2_ref, own_ref, *refs
):
    pieces, (gain_ref, shift_ref, gain2_ref, shift2_ref, inside_ref, flat_ref, expand_ref) = refs[:6], refs[6:13]
    x_ref, c_ref, out_ref, frame = refs[13:]
    half = CELLS // 2
    for off in range(HELD):
        start = lax.rem(at_ref[0] + off, HELD) * CELLS
        for h in range(2):
            piece = own_ref[half * h : half * (h + 1), :] if off == 0 else pieces[2 * (off - 1) + h][...]
            x_ref[pl.ds(pl.multiple_of(start + half * h, half), half), :] = piece
    norm = normalizer(parts_ref[...], gain_ref[...], shift_ref[...], OWN, True)
    norm2 = normalizer(parts2_ref[...], gain2_ref[...], shift2_ref[...], OWN, True)
    taps, weights = spatial_of(flat_ref, 0), expand_of(expand_ref, 0)
    tiles = []
    for p in range(PAIRS):
        y = reduced_pair(x_ref[tile_at(2 * p), :], x_ref[tile_at(2 * p + 1), :], reduce_of(flat_ref, 0))
        y2 = convolved(y, norm, inside_ref[...], taps, frame.at[p])
        c = jnp.maximum(norm2(y2), 0.0).astype(jnp.bfloat16)
        c_ref[tile_at(p), :] = c
        expanded(c, weights, tiles)
    send_moments(out_ref, tiles)


def spatial_kernel(block, parts_ref, y_ref, gain_ref, shift_ref, inside_ref, flat_ref, y2_ref, out_ref, frame):
    norm = normalizer(parts_ref[...], gain_ref[...], shift_ref[...], HELD * OWN, True)
    taps = spatial_of(flat_ref, block)
    tiles = []
    for p in range(PAIRS):
        y2 = convolved(y_ref[tile_at(p), :], norm, inside_ref[...], taps, frame.at[p])
        y2_ref[tile_at(p), :] = y2
        tiles += pair_moments(y2)
    send_moments(out_ref, tiles)


def expand_kernel(block, parts_ref, y_ref, gain_ref, shift_ref, expand_ref, c_ref, out_ref):
    norm = normalizer(parts_ref[...], gain_ref[...], shift_ref[...], HELD * OWN, True)
    weights = expand_of(expand_ref, block)
    tiles = []
    for p in range(PAIRS):
        c = jnp.maximum(norm(y_ref[tile_at(p), :]), 0.0).astype(jnp.bfloat16)
        c_ref[tile_at(p), :] = c
        expanded(c, weights, tiles)
    send_moments(out_ref, tiles)


def block_kernel(block, parts_ref, c_ref, gain_ref, shift_ref, x_ref, expand_ref, flat_ref, new_ref, y1_ref, out_ref):
    norm = normalizer(parts_ref[...], gain_ref[...], shift_ref[...], HELD * OWN)
    weights = expand_of(expand_ref, block)
    tiles = []
    for p in range(PAIRS):
        pair = []
        for h in range(2):
            y = dot_t(c_ref[tile_at(p), :], weights[h])
            x = x_ref[tile_at(2 * p + h), :].astype(jnp.float32)
            new = jnp.maximum(x + norm(y), 0.0).astype(jnp.bfloat16)
            new_ref[tile_at(2 * p + h), :] = new
            pair.append(new)
        y1 = reduced_pair(*pair, reduce_of(flat_ref, block + 1))
        y1_ref[tile_at(p), :] = y1
        tiles += pair_moments(y1)
    send_moments(out_ref, tiles)


def last_kernel(block, at_ref, parts_ref, c_ref, gain_ref, shift_ref, x_ref, expand_ref, new_ref, out_ref):
    norm = normalizer(parts_ref[...], gain_ref[...], shift_ref[...], HELD * OWN)
    weights = expand_of(expand_ref, block)
    sums = []
    for k in range(HELD):
        c = c_ref[tile_at(k // 2), :][:OWN_ROWS]
        y = dot_t(c, weights[k % 2])
        top = x_ref[tile_at(k), :][:OWN_ROWS].astype(jnp.float32) + norm(y)
        new = jnp.maximum(top, 0.0).astype(jnp.bfloat16)

        @pl.when(at_ref[0] == k)
        def _():
            for row in range(TILE):
                new_ref[row] = new[SIDE * row : SIDE * row + TILE]

        by_col = jnp.sum(new.astype(jnp.float32).reshape(TILE, SIDE, FEAT), axis=0)
        sums.append(jnp.sum(by_col[:TILE], axis=0, keepdims=True))
    send(out_ref, jnp.concatenate(sums, axis=1))


def call(kernel, outs, *args, scratch=(), smem=0):
    return pl.pallas_call(
        kernel,
        out_shape=[jax.ShapeDtypeStruct(s, d) for s, d in outs],
        in_specs=[SM] * smem + [VM] * (len(args) - smem),
        out_specs=[VM] * len(outs),
        scratch_shapes=list(scratch),
        compiler_params=PARAMS,
    )(*args)


def tile_frame(features, sy, sx):
    own = features[0]
    cols = jnp.where(sx == 0, own[:, TILE - HALO :], own[:, :HALO])
    rows = jnp.where(sy == 0, own[TILE - HALO :], own[:HALO])
    corner = jnp.where(sx == 0, rows[:, TILE - HALO :], rows[:, :HALO])
    cols = lax.ppermute(cols, "sx", [(0, 1), (1, 0)])
    rows = lax.ppermute(rows, "sy", [(0, 1), (1, 0)])
    corner = lax.ppermute(corner, ("sy", "sx"), [(i, 3 - i) for i in range(4)])
    right = jnp.concatenate([cols, corner], axis=0)
    right = jnp.where(sx == 1, jnp.concatenate([right[1:], right[:1]], axis=0), right)
    left = jnp.concatenate([own, rows], axis=0)
    return jnp.concatenate([left, right], axis=1).reshape(CELLS, FEAT)


def inside_image(sy, sx):
    cell = lax.broadcasted_iota(jnp.int32, (CELLS, 2 * MID), 0)
    col = cell % SIDE
    row = ((cell + jnp.where((sx == 1) & (col > TILE), SIDE, 0)) // SIDE) % SIDE
    inside = (row != SIDE - 1 - 3 * sy) & (col != SIDE - 1 - 3 * sx)
    return inside.astype(jnp.float32)


def exchange(copies, axes):
    rows = lax.all_to_all(copies, axes, 0, 0, tiled=True)
    return rows if rows.shape[1] == 4 else rows.reshape(rows.shape[0], -1)


def held_tiles(own, z4):
    fore, back = [(i, (i + 1) % 4) for i in range(4)], [((i + 1) % 4, i) for i in range(4)]
    half = CELLS // 2
    top, bottom = own[:half], own[half:]
    below = [lax.ppermute(v, "z4", fore) for v in (top, bottom)]
    above = [lax.ppermute(v, "z4", back) for v in (bottom, top)]

    def finish(after):
        low, high, _ = lax.optimization_barrier((below[0], above[0], after))
        far = [lax.ppermute(low, "z4", fore), lax.ppermute(high, "z4", back)]
        return [above[1], high, *far, low, below[1]]

    return finish


def per_device(
    features,
    labels,
    grid,
    w_reduce,
    w_spatial,
    w_expand,
    w_class,
    dir_reduce,
    dir_spatial,
    dir_expand,
    dir_class,
    gain_mid,
    shift_mid,
    gain_out,
    shift_out,
):
    z4, sy, sx = (lax.axis_index(a) for a in ("z4", "sy", "sx"))
    tile = 2 * sy + sx
    alpha = (2.0 * grid.astype(jnp.float32) + 1.0 - GRID) / GRID

    with jax.named_scope("halo"):
        own = tile_frame(features, sy, sx)
        inside = inside_image(sy, sx)

    with jax.named_scope("filters"):
        def rows_of(reduce, spatial, expand):
            return jnp.concatenate(
                [
                    reduce[:, :, 0].reshape(12, MID),
                    spatial[..., 0].reshape(27, MID),
                    jnp.zeros((1, MID), jnp.bfloat16),
                    jnp.transpose(expand, (2, 0, 1)).reshape(12, MID),
                    jnp.zeros((ROWS - 52, MID), jnp.bfloat16),
                ],
                axis=0,
            )

        parts = (w_reduce, w_spatial, w_expand, dir_reduce, dir_spatial, dir_expand)
        own, parts = lax.optimization_barrier((own, parts))
        w_reduce, w_spatial, w_expand, dir_reduce, dir_spatial, dir_expand = parts
        finish = held_tiles(own, z4)
        raw = jnp.stack(
            [rows_of(w_reduce, w_spatial, w_expand)]
            + [rows_of(dir_reduce[k], dir_spatial[k], dir_expand[k]) for k in range(2)]
        ).astype(jnp.float32)
        (mine,) = call(
            filter_kernel, [((ROWS, MID), jnp.bfloat16)], grid, raw, smem=1
        )
        quarter = lax.dynamic_slice(mine[:FLAT].reshape(TILES, 5, 128), (tile, 0, 0), (1, 5, 128))
        expand = lax.dynamic_slice(mine[FLAT : FLAT + 12].reshape(TILES, 3 * MID), (tile, 0), (1, 3 * MID))
        pick = lambda v: lax.dynamic_slice(v, (tile, 0), (1, CLASSES))
        rows = jnp.concatenate([pick(w_class), pick(dir_class[0]), pick(dir_class[1])], axis=0)
        rows = jnp.pad(rows, ((0, 0), (0, 64 * CLASS_PART - CLASSES))).reshape(3, 64, CLASS_PART)
        rows = jnp.moveaxis(rows, 0, 1).reshape(64, 3 * CLASS_PART)
        tag = jnp.concatenate([labels // 32, labels % 32]).astype(jnp.bfloat16)
        tag = jnp.pad(tag, (0, MID - 2 - 3 * CLASS_PART))
        rows = jnp.concatenate(
            [jnp.broadcast_to(expand, (64, 3 * MID)), rows, jnp.broadcast_to(tag, (64, tag.size))], axis=1
        )
        rows = jnp.broadcast_to(rows[None], (4, 64, 2 * 128)).reshape(256, 2, 128)
        quarter = jnp.broadcast_to(quarter, (256, 5, 128))
        copies = jnp.concatenate([rows, quarter, jnp.zeros((256, 1, 128), jnp.bfloat16)], axis=1)
        every = lax.all_to_all(copies, ALL, 0, 0, tiled=True)
        first = every.reshape(64, TILES, 8, 128)[:, 0, 2:4, :].reshape(MID, FEAT)
        (sent,) = call(reduce_kernel, [((256, 1, 128), jnp.float32)], own, first)
        pieces = finish(sent)
        ready, every = lax.optimization_barrier((sent, every))
        expand = every[:, :2, :].reshape(256, 256)
        flat = every[:, 2:7, :].reshape(64, FLAT * MID)

    with jax.named_scope("class"):
        rows = expand[:, 3 * MID :]
        high, low = (rows[::TILES, 3 * CLASS_PART + k].astype(jnp.int32) for k in range(2))
        table = high * 32 + low
        tags = table.reshape(4, 16).T.reshape(IMAGES)
        raw = rows[:, : 3 * CLASS_PART].astype(jnp.float32).reshape(FEAT, 3, CLASS_PART)
        norms = jnp.sum(raw * raw, axis=0)
        base = jnp.sqrt(norms[0])
        p_class = raw[:, 0]
        for k in range(2):
            p_class = p_class + alpha[k] * (base / jnp.sqrt(norms[k + 1] + EPS_NORM)) * raw[:, k + 1]
        p_class = p_class.astype(jnp.bfloat16)

    row = lambda v: v.reshape(1, -1)
    mids = [[(row(gain_mid[b, k]), row(shift_mid[b, k])) for k in range(2)] for b in range(BLOCKS)]
    outs = [(row(gain_out[b]), row(shift_out[b])) for b in range(BLOCKS)]
    place = z4.astype(jnp.int32).reshape(1)
    parts = exchange(sent, ALL)
    early = (parts, expand, flat, p_class, tags, inside, mids, outs, place)
    parts, expand, flat, p_class, tags, inside, mids, outs, place = lax.optimization_barrier(early)
    frames = lambda n: [pltpu.VMEM((n, CELLS + 2 * SIDE, 6 * MID), jnp.bfloat16)]
    pairs_of = lambda kind: ((PAIRS * CELLS, 2 * MID), kind)
    held = ((HELD * CELLS, FEAT), jnp.bfloat16)
    narrow, wide = ((64, 1, 128), jnp.float32), ((64, 4, 128), jnp.float32)
    for b in range(BLOCKS):
        with jax.named_scope(f"block_{b}"):
            if b == 0:
                (sent,) = call(
                    first_own_kernel, [((256, 1, 128), jnp.float32)],
                    parts, own, *mids[0][0], inside, flat, scratch=frames(1),
                )
                x, c, sent = call(
                    first_expand_kernel, [held, pairs_of(jnp.bfloat16), wide],
                    place, parts, exchange(sent, ALL), own, *pieces, *mids[0][0], *mids[0][1],
                    inside, flat, expand, scratch=frames(PAIRS), smem=1,
                )
            else:
                y2, sent = call(
                    functools.partial(spatial_kernel, b), [pairs_of(jnp.float32), narrow],
                    exchange(sent, GROUP), y1, *mids[b][0], inside, flat, scratch=frames(PAIRS),
                )
                c, sent = call(
                    functools.partial(expand_kernel, b), [pairs_of(jnp.bfloat16), wide],
                    exchange(sent, GROUP), y2, *mids[b][1], expand,
                )
            args = (exchange(sent, GROUP), c, *outs[b], x, expand)
            if b < BLOCKS - 1:
                x, y1, sent = call(
                    functools.partial(block_kernel, b), [held, pairs_of(jnp.float32), narrow], *args, flat
                )
            else:
                section, pooled = call(
                    functools.partial(last_kernel, b),
                    [((TILE, TILE, FEAT), jnp.bfloat16), ((64, 8, 128), jnp.float32)],
                    place, *args, smem=1,
                )
    with jax.named_scope("loss"):
        every = exchange(pooled, GROUP).reshape(16, TILES, HELD, FEAT)
        pooled = (jnp.sum(every, axis=1) / (OWN * TILES)).astype(jnp.bfloat16).reshape(IMAGES, FEAT)
        logits = jnp.dot(pooled, p_class, preferred_element_type=jnp.float32)
        classes = lax.broadcasted_iota(jnp.int32, logits.shape, 1) + CLASS_PART * lax.axis_index(GROUP)
        terms = jnp.sum(jnp.where(classes < CLASSES, jnp.exp(logits), 0.0), axis=1)
        picked = jnp.sum(jnp.where(classes == tags[:, None], logits, 0.0), axis=1)
        terms = jnp.broadcast_to(jnp.concatenate([terms, picked]), (64, 1, 128))
        total = jnp.sum(exchange(terms, GROUP), axis=0)
        losses = jnp.log(total[:IMAGES]) - total[IMAGES:]
        mean_loss = jnp.sum(losses) / IMAGES
        mine = HELD * lax.axis_index(("z2", "y", "xh")) + z4
        image_loss = lax.dynamic_slice(losses, (mine,), (1,))
    return section[None], image_loss, mean_loss


def solution(mesh):
    split = Mesh(
        mesh.devices.reshape(4, 2, 4, 2, mesh.shape["sy"], mesh.shape["sx"]), ALL
    )
    tiles = P(DP, "sy", "sx", None)
    return jax.shard_map(
        per_device,
        mesh=split,
        in_specs=(
            tiles,
            P(DP),
            P(),
            P(None, None, DP),
            P(None, None, None, None, DP),
            P(None, None, DP),
            P(DP, None),
            P(None, None, None, DP),
            P(None, None, None, None, None, DP),
            P(None, None, None, DP),
            P(None, DP, None),
            P(),
            P(),
            P(),
            P(),
        ),
        out_specs=(tiles, P(DP), P()),
        check_vma=False,
    )
```

```python
import functools

import jax
import jax.numpy as jnp
from jax import lax
from jax.experimental import pallas as pl
from jax.experimental.pallas import tpu as pltpu
from jax.sharding import Mesh
from jax.sharding import PartitionSpec as P

BLOCKS = 3
GRID = 50
EPS_NORM = 1e-06
EPS_BN = 1e-05
FEAT = 256
MID = 64
CLASSES = 1000
TILE = 28
OWN = TILE * TILE
SIDE = 32
CELLS = SIDE * SIDE
OWN_ROWS = TILE * SIDE
HALO = SIDE - TILE
DP = ("z4", "z2", "y", "xh")
GROUP = ("z2", "y", "xh", "sy", "sx")
ALL = ("z4",) + GROUP
TILES = 4
HELD = 4
PAIRS = HELD // 2
IMAGES = 64
CLASS_PART = 16

ROWS = 56
FLAT = 40

PARAMS = pltpu.CompilerParams(vmem_limit_bytes=16 * 1024 * 1024)
VM = pl.BlockSpec(memory_space=pltpu.VMEM)
SM = pl.BlockSpec(memory_space=pltpu.SMEM)


def dot_t(left, right):
    return lax.dot_general(
        left, right, (((1,), (1,)), ((), ())), preferred_element_type=jnp.float32
    )


def tile_moments(y):
    cells = y[:OWN_ROWS].reshape(TILE, SIDE, y.shape[1])
    mean = jnp.sum(jnp.sum(cells, axis=0)[:TILE], axis=0, keepdims=True) * (1.0 / OWN)
    off = cells - mean[None]
    return mean, jnp.sum(jnp.sum(off * off, axis=0)[:TILE], axis=0, keepdims=True)


def halves(pair):
    return [pair[:, :MID], pair[:, MID:]]


def merged(means, squares, cells):
    mean = functools.reduce(jnp.add, means) * (1.0 / len(means))
    total = functools.reduce(jnp.add, squares)
    for m in means:
        total = total + cells * ((m - mean) * (m - mean))
    return mean, total


def normalizer(parts, gain, shift, cells, pairs=False):
    count = parts.shape[0]
    split = (lambda v: (v[:, :2], v[:, 2:])) if parts.ndim == 3 else (lambda v: (v[:, :MID], v[:, MID:]))
    means, squares = split(parts)
    mean = jnp.sum(means, axis=0, keepdims=True) * (1.0 / count)
    off = means - mean
    var = jnp.sum(squares + cells * (off * off), axis=0, keepdims=True) * (1.0 / (cells * count))
    if parts.ndim == 3:
        mean, var = (jnp.concatenate([v[0, :1], v[0, 1:]], axis=1) for v in (mean, var))
    scale = lax.rsqrt(var + EPS_BN) * gain
    if pairs:
        mean, scale, shift = (jnp.concatenate([v, v], axis=1) for v in (mean, scale, shift))
    return lambda y: (y - mean) * scale + shift


def send(out_ref, row):
    for k in range(out_ref.shape[1]):
        piece = row[:, 128 * k : 128 * (k + 1)].reshape(1, 1, 128)
        out_ref[:, k : k + 1, :] = jnp.broadcast_to(piece, (out_ref.shape[0], 1, 128))


def send_moments(out_ref, tiles):
    mean, squares = merged([t[0] for t in tiles], [t[1] for t in tiles], OWN)
    send(out_ref, jnp.concatenate([mean, squares], axis=1))


def pair_moments(pair):
    mean, squares = tile_moments(pair)
    return list(zip(halves(mean), halves(squares)))


def filters_kernel(
    grid_ref, label_ref, tile_ref, wr_ref, dr_ref, ws_ref, ds_ref, we_ref, de_ref, wc_ref, dc_ref, out_ref, rows, flat, classes, sent
):
    alpha = [(2.0 * grid_ref[k].astype(jnp.float32) + 1.0 - GRID) / GRID for k in range(2)]
    wide = lambda v: v.astype(jnp.float32)

    def filters(base, directions, axes):
        square = lambda v: jnp.sum(v * v, axis=axes, keepdims=True)
        length = jnp.sqrt(square(base))
        value = base
        for k in range(2):
            value = value + alpha[k] * (length / jnp.sqrt(square(directions[k]) + EPS_NORM)) * directions[k]
        return value

    rows[...] = jnp.zeros_like(rows)
    both = wide(dr_ref[...])
    reduce = filters(wide(wr_ref[...]), [both[:, k, :] for k in range(2)], 1)
    for b in range(BLOCKS):
        for q in range(4):
            rows[4 * b + q : 4 * b + q + 1, :] = reduce[b : b + 1, MID * q : MID * (q + 1)]
        both = wide(ds_ref[b])
        spatial = filters(wide(ws_ref[b]), [both[:, :, k, :] for k in range(2)], (0, 1, 2))
        for i in range(3):
            rows[12 + 9 * b + 3 * i : 15 + 9 * b + 3 * i, :] = spatial[i]
        expand = filters(wide(we_ref[b]), [wide(de_ref[k, b]) for k in range(2)], 1)
        for k in range(4):
            rows[FLAT + 3 * k + b : FLAT + 3 * k + b + 1, :] = expand[k : k + 1]
    flat[0:20, :] = jnp.concatenate([rows[pl.ds(h, 20, stride=2), :] for h in range(2)], axis=1)
    tile = tile_ref[0]
    quarter = flat[pl.ds(5 * tile, 5), :]

    classes[...] = jnp.zeros_like(classes)
    classes[0:4, :CLASSES] = wide(wc_ref[...])
    for k in range(2):
        classes[4 + 4 * k : 8 + 4 * k, :CLASSES] = wide(dc_ref[k])
    sent[...] = jnp.zeros_like(sent)
    for b in range(BLOCKS):
        sent[:, MID * b : MID * (b + 1)] = jnp.broadcast_to(rows[pl.ds(FLAT + 3 * tile + b, 1), :], (64, MID))
    for a in range(3):
        row = classes[pl.ds(4 * a + tile, 1), :]
        at = 3 * MID + CLASS_PART * a
        for g in range(64):
            sent[g : g + 1, at : at + CLASS_PART] = row[:, CLASS_PART * g : CLASS_PART * (g + 1)]
    at = 3 * MID + 3 * CLASS_PART
    label = label_ref[0]
    sent[:, at : at + 1] = jnp.full((64, 1), wide(label >> 5), jnp.float32)
    sent[:, at + 1 : at + 2] = jnp.full((64, 1), wide(label & 31), jnp.float32)
    pieces = [sent[:, :128].reshape(64, 1, 128), sent[:, 128:].reshape(64, 1, 128)]
    pieces += [jnp.broadcast_to(quarter[None], (64, 5, 128)), jnp.zeros((64, 1, 128), jnp.float32)]
    copies = jnp.concatenate(pieces, axis=1).astype(jnp.bfloat16)
    for z in range(4):
        out_ref[64 * z : 64 * (z + 1)] = copies


def reduce_kernel(x_ref, w_ref, out_ref):
    send_moments(out_ref, [tile_moments(dot_t(x_ref[...], w_ref[...]))])


def reduced_pair(first, second, w):
    zero = jnp.zeros_like(w)
    return dot_t(first, jnp.concatenate([w, zero], axis=0)) + dot_t(
        second, jnp.concatenate([zero, w], axis=0)
    )


def tile_at(k):
    return slice(CELLS * k, CELLS * (k + 1))


def reduce_of(flat_ref, block):
    return flat_ref[:, FEAT * block : FEAT * (block + 1)]


def spatial_of(flat_ref, block):
    start = FEAT * BLOCKS + 9 * MID * block
    taps = [flat_ref[:, start + MID * t : start + MID * (t + 1)] for t in range(9)]
    zero = jnp.zeros_like(taps[0])
    rows = []
    for i in range(3):
        rows.append(jnp.concatenate([v for t in taps[3 * i : 3 * i + 3] for v in (t, zero)], axis=1))
        rows.append(jnp.concatenate([v for t in taps[3 * i : 3 * i + 3] for v in (zero, t)], axis=1))
    return jnp.concatenate(rows, axis=0)


def expand_of(expand_ref, block):
    w = expand_ref[:, MID * block : MID * (block + 1)]
    zero = jnp.zeros_like(w)
    return [jnp.concatenate(v, axis=1) for v in ((w, zero), (zero, w))]


def convolved(y, norm, inside, taps):
    a = jnp.maximum(norm(y), 0.0) * inside
    sides = [v.astype(jnp.bfloat16) for v in (pltpu.roll(a, 1, 0), a, pltpu.roll(a, CELLS - 1, 0))]
    each = dot_t(jnp.concatenate(sides, axis=1), taps)
    above, here, below = (each[:, 2 * MID * i : 2 * MID * (i + 1)] for i in range(3))
    above = jnp.concatenate([above[CELLS - SIDE :], above[: CELLS - SIDE]], axis=0)
    below = jnp.concatenate([below[SIDE:], below[:SIDE]], axis=0)
    return above + here + below


def first_own_kernel(parts_ref, x_ref, gain_ref, shift_ref, inside_ref, flat_ref, out_ref):
    norm = normalizer(parts_ref[...], gain_ref[...], shift_ref[...], OWN, True)
    y = reduced_pair(x_ref[...], x_ref[...], reduce_of(flat_ref, 0))
    y2 = convolved(y, norm, inside_ref[...], spatial_of(flat_ref, 0))
    send_moments(out_ref, pair_moments(y2)[:1])


def expanded(c, pair_weights, tiles):
    for w in pair_weights:
        tiles.append(tile_moments(dot_t(c[:OWN_ROWS], w)))


def first_expand_kernel(
    at_ref, parts_ref, parts2_ref, own_ref, *refs
):
    pieces, (gain_ref, shift_ref, gain2_ref, shift2_ref, inside_ref, flat_ref, expand_ref) = refs[:6], refs[6:13]
    x_ref, c_ref, out_ref = refs[13:]
    half = CELLS // 2
    for off in range(HELD):
        start = lax.rem(at_ref[0] + off, HELD) * CELLS
        for h in range(2):
            piece = own_ref[half * h : half * (h + 1), :] if off == 0 else pieces[2 * (off - 1) + h][...]
            x_ref[pl.ds(pl.multiple_of(start + half * h, half), half), :] = piece
    norm = normalizer(parts_ref[...], gain_ref[...], shift_ref[...], OWN, True)
    norm2 = normalizer(parts2_ref[...], gain2_ref[...], shift2_ref[...], OWN, True)
    taps, weights = spatial_of(flat_ref, 0), expand_of(expand_ref, 0)
    tiles = []
    for p in range(PAIRS):
        y = reduced_pair(x_ref[tile_at(2 * p), :], x_ref[tile_at(2 * p + 1), :], reduce_of(flat_ref, 0))
        y2 = convolved(y, norm, inside_ref[...], taps)
        c = jnp.maximum(norm2(y2), 0.0).astype(jnp.bfloat16)
        c_ref[tile_at(p), :] = c
        expanded(c, weights, tiles)
    send_moments(out_ref, tiles)


def spatial_kernel(block, parts_ref, y_ref, gain_ref, shift_ref, inside_ref, flat_ref, y2_ref, out_ref):
    norm = normalizer(parts_ref[...], gain_ref[...], shift_ref[...], HELD * OWN, True)
    taps = spatial_of(flat_ref, block)
    tiles = []
    for p in range(PAIRS):
        y2 = convolved(y_ref[tile_at(p), :], norm, inside_ref[...], taps)
        y2_ref[tile_at(p), :] = y2
        tiles += pair_moments(y2)
    send_moments(out_ref, tiles)


def expand_kernel(block, parts_ref, y_ref, gain_ref, shift_ref, expand_ref, c_ref, out_ref):
    norm = normalizer(parts_ref[...], gain_ref[...], shift_ref[...], HELD * OWN, True)
    weights = expand_of(expand_ref, block)
    tiles = []
    for p in range(PAIRS):
        c = jnp.maximum(norm(y_ref[tile_at(p), :]), 0.0).astype(jnp.bfloat16)
        c_ref[tile_at(p), :] = c
        expanded(c, weights, tiles)
    send_moments(out_ref, tiles)


def block_kernel(block, parts_ref, c_ref, gain_ref, shift_ref, x_ref, expand_ref, flat_ref, new_ref, y1_ref, out_ref):
    norm = normalizer(parts_ref[...], gain_ref[...], shift_ref[...], HELD * OWN)
    weights = expand_of(expand_ref, block)
    tiles = []
    for p in range(PAIRS):
        pair = []
        for h in range(2):
            y = dot_t(c_ref[tile_at(p), :], weights[h])
            x = x_ref[tile_at(2 * p + h), :].astype(jnp.float32)
            new = jnp.maximum(x + norm(y), 0.0).astype(jnp.bfloat16)
            new_ref[tile_at(2 * p + h), :] = new
            pair.append(new)
        y1 = reduced_pair(*pair, reduce_of(flat_ref, block + 1))
        y1_ref[tile_at(p), :] = y1
        tiles += pair_moments(y1)
    send_moments(out_ref, tiles)


def last_kernel(block, at_ref, parts_ref, c_ref, gain_ref, shift_ref, x_ref, expand_ref, new_ref, out_ref):
    norm = normalizer(parts_ref[...], gain_ref[...], shift_ref[...], HELD * OWN)
    weights = expand_of(expand_ref, block)
    sums = []
    for k in range(HELD):
        c = c_ref[tile_at(k // 2), :][:OWN_ROWS]
        y = dot_t(c, weights[k % 2])
        top = x_ref[tile_at(k), :][:OWN_ROWS].astype(jnp.float32) + norm(y)
        new = jnp.maximum(top, 0.0).astype(jnp.bfloat16)

        @pl.when(at_ref[0] == k)
        def _():
            for row in range(TILE):
                new_ref[row] = new[SIDE * row : SIDE * row + TILE]

        by_col = jnp.sum(new.astype(jnp.float32).reshape(TILE, SIDE, FEAT), axis=0)
        sums.append(jnp.sum(by_col[:TILE], axis=0, keepdims=True))
    send(out_ref, jnp.concatenate(sums, axis=1))


def loss_kernel(mine_ref, parts_ref, own_ref, mean_ref):
    total = jnp.sum(parts_ref[...], axis=0, keepdims=True)
    losses = jnp.log(total[:, :IMAGES]) - total[:, IMAGES:]
    image = lax.broadcasted_iota(jnp.int32, losses.shape, 1)
    own_ref[...] = jnp.sum(jnp.where(image == mine_ref[0], losses, 0.0), axis=1, keepdims=True)
    mean_ref[...] = jnp.sum(losses, axis=1, keepdims=True) * (1.0 / IMAGES)


def call(kernel, outs, *args, scratch=(), smem=0, params=PARAMS):
    return pl.pallas_call(
        kernel,
        out_shape=[jax.ShapeDtypeStruct(s, d) for s, d in outs],
        in_specs=[SM] * smem + [VM] * (len(args) - smem),
        out_specs=[VM] * len(outs),
        scratch_shapes=list(scratch),
        compiler_params=params,
    )(*args)


def tile_frame(features, sy, sx):
    own = features[0]
    cols = jnp.where(sx == 0, own[:, TILE - HALO :], own[:, :HALO])
    rows = jnp.where(sy == 0, own[TILE - HALO :], own[:HALO])
    corner = jnp.where(sx == 0, rows[:, TILE - HALO :], rows[:, :HALO])
    cols = lax.ppermute(cols, "sx", [(0, 1), (1, 0)])
    rows = lax.ppermute(rows, "sy", [(0, 1), (1, 0)])
    corner = lax.ppermute(corner, ("sy", "sx"), [(i, 3 - i) for i in range(4)])
    right = jnp.concatenate([cols, corner], axis=0)
    right = jnp.where(sx == 1, jnp.concatenate([right[1:], right[:1]], axis=0), right)
    left = jnp.concatenate([own, rows], axis=0)
    return jnp.concatenate([left, right], axis=1).reshape(CELLS, FEAT)


def inside_image(sy, sx):
    cell = lax.broadcasted_iota(jnp.int32, (CELLS, 2 * MID), 0)
    col = cell % SIDE
    row = ((cell + jnp.where((sx == 1) & (col > TILE), SIDE, 0)) // SIDE) % SIDE
    inside = (row != SIDE - 1 - 3 * sy) & (col != SIDE - 1 - 3 * sx)
    return inside.astype(jnp.float32)


def exchange(copies, axes):
    rows = lax.all_to_all(copies, axes, 0, 0, tiled=True)
    return rows if rows.shape[1] == 4 else rows.reshape(rows.shape[0], -1)


def held_tiles(own, z4):
    fore, back = [(i, (i + 1) % 4) for i in range(4)], [((i + 1) % 4, i) for i in range(4)]
    half = CELLS // 2
    top, bottom = own[:half], own[half:]
    below = [lax.ppermute(v, "z4", fore) for v in (top, bottom)]
    above = [lax.ppermute(v, "z4", back) for v in (bottom, top)]

    def finish(after):
        low, high, _ = lax.optimization_barrier((below[0], above[0], after))
        far = [lax.ppermute(low, "z4", fore), lax.ppermute(high, "z4", back)]
        return [above[1], high, *far, low, below[1]]

    return finish


def per_device(
    features,
    labels,
    grid,
    w_reduce,
    w_spatial,
    w_expand,
    w_class,
    dir_reduce,
    dir_spatial,
    dir_expand,
    dir_class,
    gain_mid,
    shift_mid,
    gain_out,
    shift_out,
):
    z4, sy, sx = (lax.axis_index(a) for a in ("z4", "sy", "sx"))
    tile = 2 * sy + sx
    with jax.named_scope("filters"):
        (copies,) = call(
            filters_kernel,
            [((256, 8, 128), jnp.bfloat16)],
            grid, labels, tile.astype(jnp.int32).reshape(1),
            w_reduce[:, :, 0], jnp.transpose(dir_reduce[..., 0], (1, 0, 2)),
            w_spatial[..., 0], jnp.transpose(dir_spatial[..., 0], (1, 2, 3, 0, 4)),
            jnp.swapaxes(w_expand, 1, 2), jnp.swapaxes(dir_expand, 2, 3),
            w_class, dir_class,
            scratch=[
                pltpu.VMEM((ROWS, MID), jnp.float32),
                pltpu.VMEM((24, 128), jnp.float32),
                pltpu.VMEM((16, 1024), jnp.float32),
                pltpu.VMEM((64, 256), jnp.float32),
            ],
            smem=3,
            params=pltpu.CompilerParams(),
        )
        copies, features = lax.optimization_barrier((copies, features))
        every = lax.all_to_all(copies, ALL, 0, 0, tiled=True)

    with jax.named_scope("halo"):
        own = tile_frame(features, sy, sx)
        finish = held_tiles(own, z4)
        inside = inside_image(sy, sx)

    with jax.named_scope("reduce"):
        first = every.reshape(64, TILES, 8, 128)[:, 0, 2:4, :].reshape(MID, FEAT)
        (sent,) = call(reduce_kernel, [((256, 1, 128), jnp.float32)], own, first)
        pieces = finish(sent)
        every, point, _ = lax.optimization_barrier((every, grid, sent))
        expand = every[:, :2, :].reshape(256, 256)
        flat = every[:, 2:7, :].reshape(64, FLAT * MID)

    with jax.named_scope("class"):
        rows = expand[:, 3 * MID :]
        high, low = (rows[::TILES, 3 * CLASS_PART + k].astype(jnp.int32) for k in range(2))
        table = high * 32 + low
        tags = table.reshape(4, 16).T.reshape(IMAGES)
        raw = rows[:, : 3 * CLASS_PART].astype(jnp.float32).reshape(FEAT, 3, CLASS_PART)
        norms = jnp.sum(raw * raw, axis=0)
        base = jnp.sqrt(norms[0])
        alpha = (2.0 * point.astype(jnp.float32) + 1.0 - GRID) / GRID
        p_class = raw[:, 0]
        for k in range(2):
            p_class = p_class + alpha[k] * (base / jnp.sqrt(norms[k + 1] + EPS_NORM)) * raw[:, k + 1]
        p_class = p_class.astype(jnp.bfloat16)

    row = lambda v: v.reshape(1, -1)
    mids = [[(row(gain_mid[b, k]), row(shift_mid[b, k])) for k in range(2)] for b in range(BLOCKS)]
    outs = [(row(gain_out[b]), row(shift_out[b])) for b in range(BLOCKS)]
    place = z4.astype(jnp.int32).reshape(1)
    parts = exchange(sent, ALL)
    mine = HELD * lax.axis_index(("z2", "y", "xh")) + z4
    mine = mine.astype(jnp.int32).reshape(1)
    early = (parts, expand, flat, p_class, tags, inside, mids, outs, place, mine)
    parts, expand, flat, p_class, tags, inside, mids, outs, place, mine = lax.optimization_barrier(early)
    pairs_of = lambda kind: ((PAIRS * CELLS, 2 * MID), kind)
    held = ((HELD * CELLS, FEAT), jnp.bfloat16)
    narrow, wide = ((64, 1, 128), jnp.float32), ((64, 4, 128), jnp.float32)
    for b in range(BLOCKS):
        with jax.named_scope(f"block_{b}"):
            if b == 0:
                (sent,) = call(
                    first_own_kernel, [((256, 1, 128), jnp.float32)],
                    parts, own, *mids[0][0], inside, flat,
                )
                x, c, sent = call(
                    first_expand_kernel, [held, pairs_of(jnp.bfloat16), wide],
                    place, parts, exchange(sent, ALL), own, *pieces, *mids[0][0], *mids[0][1],
                    inside, flat, expand, smem=1,
                )
            else:
                y2, sent = call(
                    functools.partial(spatial_kernel, b), [pairs_of(jnp.float32), narrow],
                    exchange(sent, GROUP), y1, *mids[b][0], inside, flat,
                )
                c, sent = call(
                    functools.partial(expand_kernel, b), [pairs_of(jnp.bfloat16), wide],
                    exchange(sent, GROUP), y2, *mids[b][1], expand,
                )
            args = (exchange(sent, GROUP), c, *outs[b], x, expand)
            if b < BLOCKS - 1:
                x, y1, sent = call(
                    functools.partial(block_kernel, b), [held, pairs_of(jnp.float32), narrow], *args, flat
                )
            else:
                section, pooled = call(
                    functools.partial(last_kernel, b),
                    [((TILE, TILE, FEAT), jnp.bfloat16), ((64, 8, 128), jnp.float32)],
                    place, *args, smem=1,
                )
    with jax.named_scope("loss"):
        every = exchange(pooled, GROUP).reshape(16, TILES, HELD, FEAT)
        pooled = (jnp.sum(every, axis=1) / (OWN * TILES)).astype(jnp.bfloat16).reshape(IMAGES, FEAT)
        logits = jnp.dot(pooled, p_class, preferred_element_type=jnp.float32)
        classes = lax.broadcasted_iota(jnp.int32, logits.shape, 1) + CLASS_PART * lax.axis_index(GROUP)
        terms = jnp.sum(jnp.where(classes < CLASSES, jnp.exp(logits), 0.0), axis=1)
        picked = jnp.sum(jnp.where(classes == tags[:, None], logits, 0.0), axis=1)
        terms = jnp.broadcast_to(jnp.concatenate([terms, picked]), (64, 1, 128))
        image_loss, mean_loss = call(
            loss_kernel, [((1, 1), jnp.float32)] * 2, mine, exchange(terms, GROUP), smem=1
        )
    return section[None], image_loss.reshape(1), mean_loss.reshape(())


def solution(mesh):
    split = Mesh(
        mesh.devices.reshape(4, 2, 4, 2, mesh.shape["sy"], mesh.shape["sx"]), ALL
    )
    tiles = P(DP, "sy", "sx", None)
    return jax.shard_map(
        per_device,
        mesh=split,
        in_specs=(
            tiles,
            P(DP),
            P(),
            P(None, None, DP),
            P(None, None, None, None, DP),
            P(None, None, DP),
            P(DP, None),
            P(None, None, None, DP),
            P(None, None, None, None, None, DP),
            P(None, None, None, DP),
            P(None, DP, None),
            P(),
            P(),
            P(),
            P(),
        ),
        out_specs=(tiles, P(DP), P()),
        check_vma=False,
    )
```

```python
import functools

import jax
import jax.numpy as jnp
from jax import lax
from jax.experimental import pallas as pl
from jax.experimental.pallas import tpu as pltpu
from jax.sharding import Mesh
from jax.sharding import PartitionSpec as P

BLOCKS = 3
GRID = 50
EPS_NORM = 1e-06
EPS_BN = 1e-05
FEAT = 256
MID = 64
CLASSES = 1000
TILE = 28
OWN = TILE * TILE
SIDE = 32
CELLS = SIDE * SIDE
OWN_ROWS = TILE * SIDE
HALO = SIDE - TILE
DP = ("z4", "z2", "y", "xh")
GROUP = ("z2", "y", "xh", "sy", "sx")
ALL = ("z4",) + GROUP
TILES = 4
HELD = 4
PAIRS = HELD // 2
IMAGES = 64
CLASS_PART = 16

ROWS = 56
FLAT = 40

PARAMS = pltpu.CompilerParams(vmem_limit_bytes=16 * 1024 * 1024)
VM = pl.BlockSpec(memory_space=pltpu.VMEM)
SM = pl.BlockSpec(memory_space=pltpu.SMEM)


def dot_t(left, right):
    return lax.dot_general(
        left, right, (((1,), (1,)), ((), ())), preferred_element_type=jnp.float32
    )


def tile_moments(y):
    cells = y[:OWN_ROWS].reshape(TILE, SIDE, y.shape[1])
    mean = jnp.sum(jnp.sum(cells, axis=0)[:TILE], axis=0, keepdims=True) * (1.0 / OWN)
    off = cells - mean[None]
    return mean, jnp.sum(jnp.sum(off * off, axis=0)[:TILE], axis=0, keepdims=True)


def halves(pair):
    return [pair[:, :MID], pair[:, MID:]]


def merged(means, squares, cells):
    mean = functools.reduce(jnp.add, means) * (1.0 / len(means))
    total = functools.reduce(jnp.add, squares)
    for m in means:
        total = total + cells * ((m - mean) * (m - mean))
    return mean, total


def received_moments(parts):
    if parts.dtype == jnp.float32:
        return parts
    v = parts.astype(jnp.float32)
    if v.shape[1] == 8:
        return v + pltpu.roll(v, 7, 1) + pltpu.roll(v, 6, 1)
    upper, lower = v[:, :8], v[:, 8:]
    lower = jnp.where(lax.broadcasted_iota(jnp.int32, lower.shape, 1) < 2, lower, 0.0)
    return upper + pltpu.roll(upper, 4, 1) + lower


def normalizer(parts, gain, shift, cells, pairs=False, wide=False):
    parts = received_moments(parts)
    count = parts.shape[0]
    one_row = parts.ndim == 2
    total = jnp.sum(parts, axis=0, keepdims=one_row)
    off = parts - (total * (1.0 / count) if one_row else (total * (1.0 / count))[None])
    spread = jnp.sum(off * off, axis=0, keepdims=one_row)
    if wide:
        flat = lambda v: jnp.concatenate([v[:1], v[1:2]], axis=1)
        mean, squares, spread = flat(total), flat(total[2:4]), flat(spread)
    else:
        mean, squares, spread = total[:1, :MID], total[:1, MID:], spread[:1, :MID]
    mean = mean * (1.0 / count)
    scale = lax.rsqrt((squares + cells * spread) * (1.0 / (cells * count)) + EPS_BN) * gain
    if pairs:
        mean, scale, shift = (jnp.concatenate([v, v], axis=1) for v in (mean, scale, shift))
    return lambda y: (y - mean) * scale + shift


def send(out_ref, row):
    for k in range(out_ref.shape[1]):
        piece = row[:, 128 * k : 128 * (k + 1)].reshape(1, 1, 128)
        out_ref[:, k : k + 1, :] = jnp.broadcast_to(piece, (out_ref.shape[0], 1, 128))


def send_moments(out_ref, tiles, extra=None):
    mean, squares = merged([t[0] for t in tiles], [t[1] for t in tiles], OWN)
    row = jnp.concatenate([mean, squares], axis=1)
    if extra is None:
        return send(out_ref, row)
    rows = [row[:, 128 * k : 128 * (k + 1)] for k in range(row.shape[1] // 128)]
    left = rows[0] if len(rows) == 1 else jnp.concatenate(rows, axis=0)
    pieces = []
    for k in range(3):
        if k == 2:
            left = left[: max(1, len(rows) // 2)]
        piece = left.astype(jnp.bfloat16).astype(jnp.float32)
        pieces.append(piece)
        left = left - piece
    block = jnp.concatenate(pieces + [extra], axis=0).astype(jnp.bfloat16)
    out_ref[...] = jnp.broadcast_to(block[None], (out_ref.shape[0], *block.shape))


def pair_moments(pair):
    mean, squares = tile_moments(pair)
    return list(zip(halves(mean), halves(squares)))


def filters_kernel(
    grid_ref, label_ref, tile_ref, wr_ref, dr_ref, ws_ref, ds_ref, we_ref, de_ref, wc_ref, dc_ref, out_ref, rows, flat, classes, sent
):
    alpha = [(2.0 * grid_ref[k].astype(jnp.float32) + 1.0 - GRID) / GRID for k in range(2)]
    wide = lambda v: v.astype(jnp.float32)

    def filters(base, directions, axes):
        square = lambda v: jnp.sum(v * v, axis=axes, keepdims=True)
        length = jnp.sqrt(square(base))
        value = base
        for k in range(2):
            value = value + alpha[k] * (length / jnp.sqrt(square(directions[k]) + EPS_NORM)) * directions[k]
        return value

    rows[...] = jnp.zeros_like(rows)
    both = wide(dr_ref[...])
    reduce = filters(wide(wr_ref[...]), [both[:, k, :] for k in range(2)], 1)
    for b in range(BLOCKS):
        for q in range(4):
            rows[4 * b + q : 4 * b + q + 1, :] = reduce[b : b + 1, MID * q : MID * (q + 1)]
        both = wide(ds_ref[b])
        spatial = filters(wide(ws_ref[b]), [both[:, :, k, :] for k in range(2)], (0, 1, 2))
        for i in range(3):
            rows[12 + 9 * b + 3 * i : 15 + 9 * b + 3 * i, :] = spatial[i]
        expand = filters(wide(we_ref[b]), [wide(de_ref[k, b]) for k in range(2)], 1)
        for k in range(4):
            rows[FLAT + 3 * k + b : FLAT + 3 * k + b + 1, :] = expand[k : k + 1]
    flat[0:20, :] = jnp.concatenate([rows[pl.ds(h, 20, stride=2), :] for h in range(2)], axis=1)
    tile = tile_ref[0]
    quarter = flat[pl.ds(5 * tile, 5), :]

    classes[...] = jnp.zeros_like(classes)
    classes[0:4, :CLASSES] = wide(wc_ref[...])
    for k in range(2):
        classes[4 + 4 * k : 8 + 4 * k, :CLASSES] = wide(dc_ref[k])
    sent[...] = jnp.zeros_like(sent)
    for b in range(BLOCKS):
        sent[:, MID * b : MID * (b + 1)] = jnp.broadcast_to(rows[pl.ds(FLAT + 3 * tile + b, 1), :], (64, MID))
    for a in range(3):
        row = classes[pl.ds(4 * a + tile, 1), :]
        at = 3 * MID + CLASS_PART * a
        for g in range(64):
            sent[g : g + 1, at : at + CLASS_PART] = row[:, CLASS_PART * g : CLASS_PART * (g + 1)]
    at = 3 * MID + 3 * CLASS_PART
    label = label_ref[0]
    sent[:, at : at + 1] = jnp.full((64, 1), wide(label >> 5), jnp.float32)
    sent[:, at + 1 : at + 2] = jnp.full((64, 1), wide(label & 31), jnp.float32)
    pieces = [sent[:, :128].reshape(64, 1, 128), sent[:, 128:].reshape(64, 1, 128)]
    pieces += [jnp.broadcast_to(quarter[None], (64, 5, 128)), jnp.zeros((64, 1, 128), jnp.float32)]
    copies = jnp.concatenate(pieces, axis=1).astype(jnp.bfloat16)
    for z in range(4):
        out_ref[64 * z : 64 * (z + 1)] = copies


def reduce_kernel(x_ref, w_ref, out_ref):
    send_moments(out_ref, [tile_moments(dot_t(x_ref[...], w_ref[...]))])


def reduced_pair(first, second, w):
    zero = jnp.zeros_like(w)
    return dot_t(first, jnp.concatenate([w, zero], axis=0)) + dot_t(
        second, jnp.concatenate([zero, w], axis=0)
    )


def tile_at(k):
    return slice(CELLS * k, CELLS * (k + 1))


def reduce_of(flat_ref, block):
    return flat_ref[:, FEAT * block : FEAT * (block + 1)]


def spatial_of(flat_ref, block):
    start = FEAT * BLOCKS + 9 * MID * block
    taps = [flat_ref[:, start + MID * t : start + MID * (t + 1)] for t in range(9)]
    zero = jnp.zeros_like(taps[0])
    rows = []
    for i in range(3):
        rows.append(jnp.concatenate([v for t in taps[3 * i : 3 * i + 3] for v in (t, zero)], axis=1))
        rows.append(jnp.concatenate([v for t in taps[3 * i : 3 * i + 3] for v in (zero, t)], axis=1))
    return jnp.concatenate(rows, axis=0)


def expand_of(expand_ref, block):
    w = expand_ref[:, MID * block : MID * (block + 1)]
    zero = jnp.zeros_like(w)
    return [jnp.concatenate(v, axis=1) for v in ((w, zero), (zero, w))]


def convolved(y, norm, inside, taps):
    a = jnp.maximum(norm(y), 0.0) * inside
    sides = [v.astype(jnp.bfloat16) for v in (pltpu.roll(a, 1, 0), a, pltpu.roll(a, CELLS - 1, 0))]
    each = dot_t(jnp.concatenate(sides, axis=1), taps)
    above, here, below = (each[:, 2 * MID * i : 2 * MID * (i + 1)] for i in range(3))
    above = jnp.concatenate([above[CELLS - SIDE :], above[: CELLS - SIDE]], axis=0)
    below = jnp.concatenate([below[SIDE:], below[:SIDE]], axis=0)
    return above + here + below


def first_own_kernel(parts_ref, x_ref, gain_ref, shift_ref, inside_ref, flat_ref, out_ref):
    norm = normalizer(parts_ref[...], gain_ref[...], shift_ref[...], OWN, True)
    y = reduced_pair(x_ref[...], x_ref[...], reduce_of(flat_ref, 0))
    y2 = convolved(y, norm, inside_ref[...], spatial_of(flat_ref, 0))
    send_moments(out_ref, pair_moments(y2)[:1])


def expanded(c, pair_weights, tiles):
    for w in pair_weights:
        tiles.append(tile_moments(dot_t(c[:OWN_ROWS], w)))


def first_expand_kernel(
    span, at_ref, parts_ref, parts2_ref, own_ref, *refs
):
    pieces, (gain_ref, shift_ref, gain2_ref, shift2_ref, inside_ref, flat_ref, expand_ref, extra_ref) = refs[:6], refs[6:14]
    x_ref, c_ref, out_ref = refs[14:]
    half = CELLS // 2
    for off in range(HELD):
        start = lax.rem(at_ref[0] + off, HELD) * CELLS
        for h in range(2):
            piece = own_ref[half * h : half * (h + 1), :] if off == 0 else pieces[2 * (off - 1) + h][...]
            x_ref[pl.ds(pl.multiple_of(start + half * h, half), half), :] = piece
    norm = normalizer(parts_ref[...], gain_ref[...], shift_ref[...], OWN, True)
    norm2 = normalizer(parts2_ref[...], gain2_ref[...], shift2_ref[...], OWN, True)
    taps, weights = spatial_of(flat_ref, 0), expand_of(expand_ref, 0)
    tiles = []
    for p in range(PAIRS):
        y = reduced_pair(x_ref[tile_at(2 * p), :], x_ref[tile_at(2 * p + 1), :], reduce_of(flat_ref, 0))
        y2 = convolved(y, norm, inside_ref[...], taps)
        c = jnp.maximum(norm2(y2), 0.0).astype(jnp.bfloat16)
        c_ref[tile_at(p), :] = c
        expanded(c, weights, tiles)
    send_moments(out_ref, tiles, extra_ref[span[0] : span[1], :])


def spatial_kernel(block, span, parts_ref, y_ref, gain_ref, shift_ref, inside_ref, flat_ref, extra_ref, y2_ref, out_ref):
    norm = normalizer(parts_ref[...], gain_ref[...], shift_ref[...], HELD * OWN, True)
    taps = spatial_of(flat_ref, block)
    tiles = []
    for p in range(PAIRS):
        y2 = convolved(y_ref[tile_at(p), :], norm, inside_ref[...], taps)
        y2_ref[tile_at(p), :] = y2
        tiles += pair_moments(y2)
    send_moments(out_ref, tiles, extra_ref[span[0] : span[1], :])


def expand_kernel(block, span, parts_ref, y_ref, gain_ref, shift_ref, expand_ref, *rest):
    extra = rest[0][span[0] : span[1], :] if span else None
    c_ref, out_ref = rest[-2:]
    norm = normalizer(parts_ref[...], gain_ref[...], shift_ref[...], HELD * OWN, True)
    weights = expand_of(expand_ref, block)
    tiles = []
    for p in range(PAIRS):
        c = jnp.maximum(norm(y_ref[tile_at(p), :]), 0.0).astype(jnp.bfloat16)
        c_ref[tile_at(p), :] = c
        expanded(c, weights, tiles)
    send_moments(out_ref, tiles, extra)


def block_kernel(block, span, parts_ref, c_ref, gain_ref, shift_ref, x_ref, expand_ref, flat_ref, extra_ref, new_ref, y1_ref, out_ref):
    norm = normalizer(parts_ref[...], gain_ref[...], shift_ref[...], HELD * OWN, wide=True)
    weights = expand_of(expand_ref, block)
    tiles = []
    for p in range(PAIRS):
        pair = []
        for h in range(2):
            y = dot_t(c_ref[tile_at(p), :], weights[h])
            x = x_ref[tile_at(2 * p + h), :].astype(jnp.float32)
            new = jnp.maximum(x + norm(y), 0.0).astype(jnp.bfloat16)
            new_ref[tile_at(2 * p + h), :] = new
            pair.append(new)
        y1 = reduced_pair(*pair, reduce_of(flat_ref, block + 1))
        y1_ref[tile_at(p), :] = y1
        tiles += pair_moments(y1)
    send_moments(out_ref, tiles, extra_ref[span[0] : span[1], :])


def last_kernel(block, at_ref, parts_ref, c_ref, gain_ref, shift_ref, x_ref, expand_ref, new_ref, out_ref):
    norm = normalizer(parts_ref[...], gain_ref[...], shift_ref[...], HELD * OWN, wide=True)
    weights = expand_of(expand_ref, block)
    sums = []
    for k in range(HELD):
        c = c_ref[tile_at(k // 2), :][:OWN_ROWS]
        y = dot_t(c, weights[k % 2])
        top = x_ref[tile_at(k), :][:OWN_ROWS].astype(jnp.float32) + norm(y)
        new = jnp.maximum(top, 0.0).astype(jnp.bfloat16)

        @pl.when(at_ref[0] == k)
        def _():
            for row in range(TILE):
                new_ref[row] = new[SIDE * row : SIDE * row + TILE]

        by_col = jnp.sum(new.astype(jnp.float32).reshape(TILE, SIDE, FEAT), axis=0)
        sums.append(jnp.sum(by_col[:TILE], axis=0, keepdims=True))
    send(out_ref, jnp.concatenate(sums, axis=1))


def loss_kernel(mine_ref, pooled_ref, class_ref, tag_ref, own_ref, mean_ref):
    logits = dot_t(pooled_ref[...], class_ref[...])
    classes = lax.broadcasted_iota(jnp.int32, logits.shape, 1)
    summed = jnp.sum(jnp.where(classes < CLASSES, jnp.exp(logits), 0.0), axis=1, keepdims=True)
    picked = jnp.sum(jnp.where(classes == tag_ref[...], logits, 0.0), axis=1, keepdims=True)
    losses = jnp.log(summed) - picked
    image = lax.broadcasted_iota(jnp.int32, losses.shape, 0)
    own_ref[...] = jnp.sum(jnp.where(image == mine_ref[0], losses, 0.0), axis=0, keepdims=True)
    mean_ref[...] = jnp.sum(losses, axis=0, keepdims=True) * (1.0 / IMAGES)


def call(kernel, outs, *args, scratch=(), smem=0, params=PARAMS):
    return pl.pallas_call(
        kernel,
        out_shape=[jax.ShapeDtypeStruct(s, d) for s, d in outs],
        in_specs=[SM] * smem + [VM] * (len(args) - smem),
        out_specs=[VM] * len(outs),
        scratch_shapes=list(scratch),
        compiler_params=params,
    )(*args)


def tile_frame(features, sy, sx):
    own = features[0]
    cols = jnp.where(sx == 0, own[:, TILE - HALO :], own[:, :HALO])
    rows = jnp.where(sy == 0, own[TILE - HALO :], own[:HALO])
    corner = jnp.where(sx == 0, rows[:, TILE - HALO :], rows[:, :HALO])
    cols = lax.ppermute(cols, "sx", [(0, 1), (1, 0)])
    rows = lax.ppermute(rows, "sy", [(0, 1), (1, 0)])
    corner = lax.ppermute(corner, ("sy", "sx"), [(i, 3 - i) for i in range(4)])
    right = jnp.concatenate([cols, corner], axis=0)
    right = jnp.where(sx == 1, jnp.concatenate([right[1:], right[:1]], axis=0), right)
    left = jnp.concatenate([own, rows], axis=0)
    return jnp.concatenate([left, right], axis=1).reshape(CELLS, FEAT)


def inside_image(sy, sx):
    cell = lax.broadcasted_iota(jnp.int32, (CELLS, 2 * MID), 0)
    col = cell % SIDE
    row = ((cell + jnp.where((sx == 1) & (col > TILE), SIDE, 0)) // SIDE) % SIDE
    inside = (row != SIDE - 1 - 3 * sy) & (col != SIDE - 1 - 3 * sx)
    return inside.astype(jnp.float32)


def exchange(copies, axes):
    rows = lax.all_to_all(copies, axes, 0, 0, tiled=True)
    return rows if rows.shape[1] > 1 else rows.reshape(rows.shape[0], -1)


def held_tiles(own, z4):
    fore, back = [(i, (i + 1) % 4) for i in range(4)], [((i + 1) % 4, i) for i in range(4)]
    half = CELLS // 2
    top, bottom = own[:half], own[half:]
    below = [lax.ppermute(v, "z4", fore) for v in (top, bottom)]
    above = [lax.ppermute(v, "z4", back) for v in (bottom, top)]

    def finish(after):
        low, high, _ = lax.optimization_barrier((below[0], above[0], after))
        far = [lax.ppermute(low, "z4", fore), lax.ppermute(high, "z4", back)]
        return [above[1], high, *far, low, below[1]]

    return finish


def per_device(
    features,
    labels,
    grid,
    w_reduce,
    w_spatial,
    w_expand,
    w_class,
    dir_reduce,
    dir_spatial,
    dir_expand,
    dir_class,
    gain_mid,
    shift_mid,
    gain_out,
    shift_out,
):
    z4, sy, sx = (lax.axis_index(a) for a in ("z4", "sy", "sx"))
    tile = 2 * sy + sx
    at = jnp.stack([sy, sx]).astype(jnp.int32)
    with jax.named_scope("filters"):
        (copies,) = call(
            filters_kernel,
            [((256, 8, 128), jnp.bfloat16)],
            grid, labels, tile.astype(jnp.int32).reshape(1),
            w_reduce[:, :, 0], jnp.transpose(dir_reduce[..., 0], (1, 0, 2)),
            w_spatial[..., 0], jnp.transpose(dir_spatial[..., 0], (1, 2, 3, 0, 4)),
            jnp.swapaxes(w_expand, 1, 2), jnp.swapaxes(dir_expand, 2, 3),
            w_class, dir_class,
            scratch=[
                pltpu.VMEM((ROWS, MID), jnp.float32),
                pltpu.VMEM((24, 128), jnp.float32),
                pltpu.VMEM((16, 1024), jnp.float32),
                pltpu.VMEM((64, 256), jnp.float32),
            ],
            smem=3,
            params=pltpu.CompilerParams(),
        )
        small = lax.ppermute(copies[0, 7:], "sx", [(0, 1), (1, 0)])
        features, small = lax.optimization_barrier((features, small))
        at = at + small[0, :2].astype(jnp.int32)
        every = lax.all_to_all(copies, ALL, 0, 0, tiled=True)

    with jax.named_scope("halo"):
        own = tile_frame(features, sy, sx)
        finish = held_tiles(own, z4)

    with jax.named_scope("reduce"):
        first = every.reshape(64, TILES, 8, 128)[:, 0, 2:4, :].reshape(MID, FEAT)
        (sent,) = call(reduce_kernel, [((256, 1, 128), jnp.float32)], own, first)
        pieces = finish(sent)
        later = (every, grid, gain_mid, shift_mid, gain_out, shift_out, at, sent)
        every, point, gain_mid, shift_mid, gain_out, shift_out, at, _ = lax.optimization_barrier(later)
        inside = inside_image(at[0], at[1])
        expand = every[:, :2, :].reshape(256, 256)
        flat = every[:, 2:7, :].reshape(64, FLAT * MID)

    with jax.named_scope("class"):
        rows = expand[:, 3 * MID :]
        high, low = (rows[::TILES, 3 * CLASS_PART + k].astype(jnp.int32) for k in range(2))
        table = high * 32 + low
        tags = table.reshape(4, 16).T.reshape(IMAGES)
        raw = rows[:, : 3 * CLASS_PART].astype(jnp.float32).reshape(FEAT, 3, CLASS_PART)
        norms = jnp.sum(raw * raw, axis=0)
        base = jnp.sqrt(norms[0])
        alpha = (2.0 * point.astype(jnp.float32) + 1.0 - GRID) / GRID
        p_class = raw[:, 0]
        for k in range(2):
            p_class = p_class + alpha[k] * (base / jnp.sqrt(norms[k + 1] + EPS_NORM)) * raw[:, k + 1]
        p_class = p_class.astype(jnp.bfloat16).astype(jnp.float32).T.reshape(2 * CLASS_PART, 128)

    row = lambda v: v.reshape(1, -1)
    mids = [[(row(gain_mid[b, k]), row(shift_mid[b, k])) for k in range(2)] for b in range(BLOCKS)]
    outs = [(row(gain_out[b]), row(shift_out[b])) for b in range(BLOCKS)]
    place = z4.astype(jnp.int32).reshape(1)
    parts = exchange(sent, ALL)
    mine = HELD * lax.axis_index(("z2", "y", "xh")) + z4
    mine = mine.astype(jnp.int32).reshape(1)
    early = (parts, expand, flat, p_class, tags, inside, mids, outs, place, mine)
    parts, expand, flat, p_class, tags, inside, mids, outs, place, mine = lax.optimization_barrier(early)
    pairs_of = lambda kind: ((PAIRS * CELLS, 2 * MID), kind)
    held = ((HELD * CELLS, FEAT), jnp.bfloat16)
    narrow, wide = ((64, 8, 128), jnp.bfloat16), ((64, 16, 128), jnp.bfloat16)
    spans = [(0, 6), (6, 11), (11, 16), (16, 22), (22, 27), (27, 32)]
    received = []
    for b in range(BLOCKS):
        with jax.named_scope(f"block_{b}"):
            if b == 0:
                (sent,) = call(
                    first_own_kernel, [((256, 1, 128), jnp.float32)],
                    parts, own, *mids[0][0], inside, flat,
                )
                x, c, sent = call(
                    functools.partial(first_expand_kernel, spans.pop(0)), [held, pairs_of(jnp.bfloat16), wide],
                    place, parts, exchange(sent, ALL), own, *pieces, *mids[0][0], *mids[0][1],
                    inside, flat, expand, p_class, smem=1,
                )
                parts = exchange(sent, GROUP)
                received.append((parts, 10))
            else:
                y2, sent = call(
                    functools.partial(spatial_kernel, b, spans.pop(0)), [pairs_of(jnp.float32), narrow],
                    parts, y1, *mids[b][0], inside, flat, p_class,
                )
                parts = exchange(sent, GROUP)
                received.append((parts, 3))
                last = b == BLOCKS - 1
                c, sent = call(
                    functools.partial(expand_kernel, b, None if last else spans.pop(0)),
                    [pairs_of(jnp.bfloat16), ((64, 4, 128), jnp.float32) if last else wide],
                    parts, y2, *mids[b][1], expand, *([] if last else [p_class]),
                )
                parts = exchange(sent, GROUP)
                if not last:
                    received.append((parts, 10))
            args = (parts, c, *outs[b], x, expand)
            if b < BLOCKS - 1:
                x, y1, sent = call(
                    functools.partial(block_kernel, b, spans.pop(0)), [held, pairs_of(jnp.float32), narrow],
                    *args, flat, p_class,
                )
                parts = exchange(sent, GROUP)
                received.append((parts, 3))
            else:
                section, sent = call(
                    functools.partial(last_kernel, b),
                    [((TILE, TILE, FEAT), jnp.bfloat16), ((64, 8, 128), jnp.float32)],
                    place, *args, smem=1,
                )
    with jax.named_scope("loss"):
        pooled = exchange(sent, GROUP).reshape(16, TILES, HELD, FEAT)
        pooled = (jnp.sum(pooled, axis=1) / (OWN * TILES)).astype(jnp.bfloat16).reshape(IMAGES, FEAT)
        arrays, _ = lax.optimization_barrier(([v for v, _ in received], sent))
        arrays = [v[:, start:] for v, (_, start) in zip(arrays, received)]
        classes = jnp.concatenate(arrays, axis=1).reshape(64 * CLASS_PART, FEAT)
        image_loss, mean_loss = call(
            loss_kernel, [((1, 1), jnp.float32)] * 2, mine, pooled, classes, tags.reshape(IMAGES, 1), smem=1
        )
    return section[None], image_loss.reshape(1), mean_loss.reshape(())


def solution(mesh):
    split = Mesh(
        mesh.devices.reshape(4, 2, 4, 2, mesh.shape["sy"], mesh.shape["sx"]), ALL
    )
    tiles = P(DP, "sy", "sx", None)
    return jax.shard_map(
        per_device,
        mesh=split,
        in_specs=(
            tiles,
            P(DP),
            P(),
            P(None, None, DP),
            P(None, None, None, None, DP),
            P(None, None, DP),
            P(DP, None),
            P(None, None, None, DP),
            P(None, None, None, None, None, DP),
            P(None, None, None, DP),
            P(None, DP, None),
            P(),
            P(),
            P(),
            P(),
        ),
        out_specs=(tiles, P(DP), P()),
        check_vma=False,
    )
```

```python
import functools

import jax
import jax.numpy as jnp
from jax import lax
from jax.experimental import pallas as pl
from jax.experimental.pallas import tpu as pltpu
from jax.sharding import Mesh
from jax.sharding import PartitionSpec as P

BLOCKS = 3
GRID = 50
EPS_NORM = 1e-06
EPS_BN = 1e-05
FEAT = 256
MID = 64
CLASSES = 1000
TILE = 28
OWN = TILE * TILE
SIDE = 32
CELLS = SIDE * SIDE
OWN_ROWS = TILE * SIDE
HALO = SIDE - TILE
DP = ("z4", "z2", "y", "xh")
GROUP = ("z2", "y", "xh", "sy", "sx")
ALL = ("z4",) + GROUP
TILES = 4
HELD = 4
PAIRS = HELD // 2
IMAGES = 64
CLASS_PART = 16

ROWS = 56
FLAT = 40

PARAMS = pltpu.CompilerParams(vmem_limit_bytes=16 * 1024 * 1024)
VM = pl.BlockSpec(memory_space=pltpu.VMEM)
SM = pl.BlockSpec(memory_space=pltpu.SMEM)


def dot_t(left, right):
    return lax.dot_general(
        left, right, (((1,), (1,)), ((), ())), preferred_element_type=jnp.float32
    )


def tile_moments(y):
    cells = y[:OWN_ROWS].reshape(TILE, SIDE, y.shape[1])
    mean = jnp.sum(jnp.sum(cells, axis=0)[:TILE], axis=0, keepdims=True) * (1.0 / OWN)
    off = cells - mean[None]
    return mean, jnp.sum(jnp.sum(off * off, axis=0)[:TILE], axis=0, keepdims=True)


def halves(pair):
    return [pair[:, :MID], pair[:, MID:]]


def merged(means, squares, cells):
    mean = functools.reduce(jnp.add, means) * (1.0 / len(means))
    total = functools.reduce(jnp.add, squares)
    for m in means:
        total = total + cells * ((m - mean) * (m - mean))
    return mean, total


def received_moments(parts):
    if parts.dtype == jnp.float32:
        return parts
    v = parts.astype(jnp.float32)
    if v.shape[1] == 8:
        return v + pltpu.roll(v, 7, 1) + pltpu.roll(v, 6, 1)
    upper, lower = v[:, :8], v[:, 8:]
    lower = jnp.where(lax.broadcasted_iota(jnp.int32, lower.shape, 1) < 2, lower, 0.0)
    return upper + pltpu.roll(upper, 4, 1) + lower


def normalizer(parts, gain, shift, cells, pairs=False, wide=False):
    parts = received_moments(parts)
    count = parts.shape[0]
    one_row = parts.ndim == 2
    total = jnp.sum(parts, axis=0, keepdims=one_row)
    off = parts - (total * (1.0 / count) if one_row else (total * (1.0 / count))[None])
    spread = jnp.sum(off * off, axis=0, keepdims=one_row)
    if wide:
        flat = lambda v: jnp.concatenate([v[:1], v[1:2]], axis=1)
        mean, squares, spread = flat(total), flat(total[2:4]), flat(spread)
    else:
        mean, squares, spread = total[:1, :MID], total[:1, MID:], spread[:1, :MID]
    mean = mean * (1.0 / count)
    scale = lax.rsqrt((squares + cells * spread) * (1.0 / (cells * count)) + EPS_BN) * gain
    if pairs:
        mean, scale, shift = (jnp.concatenate([v, v], axis=1) for v in (mean, scale, shift))
    return lambda y: (y - mean) * scale + shift


def send(out_ref, row):
    for k in range(out_ref.shape[1]):
        piece = row[:, 128 * k : 128 * (k + 1)].reshape(1, 1, 128)
        out_ref[:, k : k + 1, :] = jnp.broadcast_to(piece, (out_ref.shape[0], 1, 128))


def send_moments(out_ref, tiles, extra=None):
    mean, squares = merged([t[0] for t in tiles], [t[1] for t in tiles], OWN)
    row = jnp.concatenate([mean, squares], axis=1)
    if extra is None:
        return send(out_ref, row)
    rows = [row[:, 128 * k : 128 * (k + 1)] for k in range(row.shape[1] // 128)]
    left = rows[0] if len(rows) == 1 else jnp.concatenate(rows, axis=0)
    pieces = []
    for k in range(3):
        if k == 2:
            left = left[: max(1, len(rows) // 2)]
        piece = left.astype(jnp.bfloat16).astype(jnp.float32)
        pieces.append(piece)
        left = left - piece
    block = jnp.concatenate(pieces + [extra], axis=0).astype(jnp.bfloat16)
    out_ref[...] = jnp.broadcast_to(block[None], (out_ref.shape[0], *block.shape))


def pair_moments(pair):
    mean, squares = tile_moments(pair)
    return list(zip(halves(mean), halves(squares)))


def filters_kernel(
    grid_ref, label_ref, tile_ref, wr_ref, dr_ref, ws_ref, ds_ref, we_ref, de_ref, wc_ref, dc_ref, out_ref, rows, flat, classes, sent
):
    alpha = [(2.0 * grid_ref[k].astype(jnp.float32) + 1.0 - GRID) / GRID for k in range(2)]
    wide = lambda v: v.astype(jnp.float32)

    def filters(base, directions, axes):
        square = lambda v: jnp.sum(v * v, axis=axes, keepdims=True)
        length = jnp.sqrt(square(base))
        value = base
        for k in range(2):
            value = value + alpha[k] * (length / jnp.sqrt(square(directions[k]) + EPS_NORM)) * directions[k]
        return value

    rows[...] = jnp.zeros_like(rows)
    both = wide(dr_ref[...])
    reduce = filters(wide(wr_ref[...]), [both[:, k, :] for k in range(2)], 1)
    for b in range(BLOCKS):
        for q in range(4):
            rows[4 * b + q : 4 * b + q + 1, :] = reduce[b : b + 1, MID * q : MID * (q + 1)]
        both = wide(ds_ref[b])
        spatial = filters(wide(ws_ref[b]), [both[:, :, k, :] for k in range(2)], (0, 1, 2))
        for i in range(3):
            rows[12 + 9 * b + 3 * i : 15 + 9 * b + 3 * i, :] = spatial[i]
        expand = filters(wide(we_ref[b]), [wide(de_ref[k, b]) for k in range(2)], 1)
        for k in range(4):
            rows[FLAT + 3 * k + b : FLAT + 3 * k + b + 1, :] = expand[k : k + 1]
    flat[0:20, :] = jnp.concatenate([rows[pl.ds(h, 20, stride=2), :] for h in range(2)], axis=1)
    tile = tile_ref[0]
    quarter = flat[pl.ds(5 * tile, 5), :]

    classes[...] = jnp.zeros_like(classes)
    classes[0:4, :CLASSES] = wide(wc_ref[...])
    for k in range(2):
        classes[4 + 4 * k : 8 + 4 * k, :CLASSES] = wide(dc_ref[k])
    sent[...] = jnp.zeros_like(sent)
    for b in range(BLOCKS):
        sent[:, MID * b : MID * (b + 1)] = jnp.broadcast_to(rows[pl.ds(FLAT + 3 * tile + b, 1), :], (64, MID))
    for a in range(3):
        row = classes[pl.ds(4 * a + tile, 1), :]
        at = 3 * MID + CLASS_PART * a
        for g in range(64):
            sent[g : g + 1, at : at + CLASS_PART] = row[:, CLASS_PART * g : CLASS_PART * (g + 1)]
    at = 3 * MID + 3 * CLASS_PART
    label = label_ref[0]
    sent[:, at : at + 1] = jnp.full((64, 1), wide(label >> 5), jnp.float32)
    sent[:, at + 1 : at + 2] = jnp.full((64, 1), wide(label & 31), jnp.float32)
    pieces = [sent[:, :128].reshape(64, 1, 128), sent[:, 128:].reshape(64, 1, 128)]
    pieces += [jnp.broadcast_to(quarter[None], (64, 5, 128)), jnp.zeros((64, 1, 128), jnp.float32)]
    copies = jnp.concatenate(pieces, axis=1).astype(jnp.bfloat16)
    for z in range(4):
        out_ref[64 * z : 64 * (z + 1)] = copies


def reduce_kernel(x_ref, w_ref, out_ref):
    send_moments(out_ref, [tile_moments(dot_t(x_ref[...], w_ref[...]))])


def reduced_pair(first, second, w):
    zero = jnp.zeros_like(w)
    return dot_t(first, jnp.concatenate([w, zero], axis=0)) + dot_t(
        second, jnp.concatenate([zero, w], axis=0)
    )


def tile_at(k):
    return slice(CELLS * k, CELLS * (k + 1))


def reduce_of(flat_ref, block):
    return flat_ref[:, FEAT * block : FEAT * (block + 1)]


def spatial_of(flat_ref, block):
    start = FEAT * BLOCKS + 9 * MID * block
    taps = [flat_ref[:, start + MID * t : start + MID * (t + 1)] for t in range(9)]
    zero = jnp.zeros_like(taps[0])
    rows = []
    for i in range(3):
        rows.append(jnp.concatenate([v for t in taps[3 * i : 3 * i + 3] for v in (t, zero)], axis=1))
        rows.append(jnp.concatenate([v for t in taps[3 * i : 3 * i + 3] for v in (zero, t)], axis=1))
    return jnp.concatenate(rows, axis=0)


def expand_of(expand_ref, block):
    w = expand_ref[:, MID * block : MID * (block + 1)]
    zero = jnp.zeros_like(w)
    return [jnp.concatenate(v, axis=1) for v in ((w, zero), (zero, w))]


def convolved(y, norm, inside, taps):
    a = jnp.maximum(norm(y), 0.0) * inside
    sides = [v.astype(jnp.bfloat16) for v in (pltpu.roll(a, 1, 0), a, pltpu.roll(a, CELLS - 1, 0))]
    each = dot_t(jnp.concatenate(sides, axis=1), taps)
    above, here, below = (each[:, 2 * MID * i : 2 * MID * (i + 1)] for i in range(3))
    above = jnp.concatenate([above[CELLS - SIDE :], above[: CELLS - SIDE]], axis=0)
    below = jnp.concatenate([below[SIDE:], below[:SIDE]], axis=0)
    return above + here + below


def first_own_kernel(parts_ref, x_ref, gain_ref, shift_ref, inside_ref, flat_ref, out_ref):
    norm = normalizer(parts_ref[...], gain_ref[...], shift_ref[...], OWN, True)
    y = reduced_pair(x_ref[...], x_ref[...], reduce_of(flat_ref, 0))
    y2 = convolved(y, norm, inside_ref[...], spatial_of(flat_ref, 0))
    send_moments(out_ref, pair_moments(y2)[:1])


def expanded(c, pair_weights, tiles):
    for w in pair_weights:
        tiles.append(tile_moments(dot_t(c[:OWN_ROWS], w)))


def first_expand_kernel(
    span, at_ref, parts_ref, parts2_ref, own_ref, *refs
):
    pieces, (gain_ref, shift_ref, gain2_ref, shift2_ref, inside_ref, flat_ref, expand_ref, extra_ref) = refs[:6], refs[6:14]
    x_ref, c_ref, out_ref = refs[14:]
    half = CELLS // 2
    for off in range(HELD):
        start = lax.rem(at_ref[0] + off, HELD) * CELLS
        for h in range(2):
            piece = own_ref[half * h : half * (h + 1), :] if off == 0 else pieces[2 * (off - 1) + h][...]
            x_ref[pl.ds(pl.multiple_of(start + half * h, half), half), :] = piece
    norm = normalizer(parts_ref[...], gain_ref[...], shift_ref[...], OWN, True)
    norm2 = normalizer(parts2_ref[...], gain2_ref[...], shift2_ref[...], OWN, True)
    taps, weights = spatial_of(flat_ref, 0), expand_of(expand_ref, 0)
    tiles = []
    for p in range(PAIRS):
        y = reduced_pair(x_ref[tile_at(2 * p), :], x_ref[tile_at(2 * p + 1), :], reduce_of(flat_ref, 0))
        y2 = convolved(y, norm, inside_ref[...], taps)
        c = jnp.maximum(norm2(y2), 0.0).astype(jnp.bfloat16)
        c_ref[tile_at(p), :] = c
        expanded(c, weights, tiles)
    send_moments(out_ref, tiles, extra_ref[span[0] : span[1], :])


def spatial_kernel(block, span, parts_ref, y_ref, gain_ref, shift_ref, inside_ref, flat_ref, extra_ref, y2_ref, out_ref):
    norm = normalizer(parts_ref[...], gain_ref[...], shift_ref[...], HELD * OWN, True)
    taps = spatial_of(flat_ref, block)
    tiles = []
    for p in range(PAIRS):
        y2 = convolved(y_ref[tile_at(p), :], norm, inside_ref[...], taps)
        y2_ref[tile_at(p), :] = y2
        tiles += pair_moments(y2)
    send_moments(out_ref, tiles, extra_ref[span[0] : span[1], :])


def expand_kernel(block, span, parts_ref, y_ref, gain_ref, shift_ref, expand_ref, *rest):
    extra = rest[0][span[0] : span[1], :] if span else None
    c_ref, out_ref = rest[-2:]
    norm = normalizer(parts_ref[...], gain_ref[...], shift_ref[...], HELD * OWN, True)
    weights = expand_of(expand_ref, block)
    tiles = []
    for p in range(PAIRS):
        c = jnp.maximum(norm(y_ref[tile_at(p), :]), 0.0).astype(jnp.bfloat16)
        c_ref[tile_at(p), :] = c
        expanded(c, weights, tiles)
    send_moments(out_ref, tiles, extra)


def block_kernel(block, span, parts_ref, c_ref, gain_ref, shift_ref, x_ref, expand_ref, flat_ref, extra_ref, new_ref, y1_ref, out_ref):
    norm = normalizer(parts_ref[...], gain_ref[...], shift_ref[...], HELD * OWN, wide=True)
    weights = expand_of(expand_ref, block)
    tiles = []
    for p in range(PAIRS):
        pair = []
        for h in range(2):
            y = dot_t(c_ref[tile_at(p), :], weights[h])
            x = x_ref[tile_at(2 * p + h), :].astype(jnp.float32)
            new = jnp.maximum(x + norm(y), 0.0).astype(jnp.bfloat16)
            new_ref[tile_at(2 * p + h), :] = new
            pair.append(new)
        y1 = reduced_pair(*pair, reduce_of(flat_ref, block + 1))
        y1_ref[tile_at(p), :] = y1
        tiles += pair_moments(y1)
    send_moments(out_ref, tiles, extra_ref[span[0] : span[1], :])


def last_kernel(block, at_ref, parts_ref, c_ref, gain_ref, shift_ref, x_ref, expand_ref, new_ref, out_ref):
    norm = normalizer(parts_ref[...], gain_ref[...], shift_ref[...], HELD * OWN, wide=True)
    weights = expand_of(expand_ref, block)
    sums = []
    for k in range(HELD):
        c = c_ref[tile_at(k // 2), :][:OWN_ROWS]
        y = dot_t(c, weights[k % 2])
        top = x_ref[tile_at(k), :][:OWN_ROWS].astype(jnp.float32) + norm(y)
        new = jnp.maximum(top, 0.0).astype(jnp.bfloat16)

        @pl.when(at_ref[0] == k)
        def _():
            for row in range(TILE):
                new_ref[row] = new[SIDE * row : SIDE * row + TILE]

        by_col = jnp.sum(new.astype(jnp.float32).reshape(TILE, SIDE, FEAT), axis=0)
        sums.append(jnp.sum(by_col[:TILE], axis=0, keepdims=True))
    send(out_ref, jnp.concatenate(sums, axis=1))


def loss_kernel(mine_ref, pooled_ref, class_ref, tag_ref, own_ref, mean_ref):
    logits = dot_t(pooled_ref[...], class_ref[...])
    classes = lax.broadcasted_iota(jnp.int32, logits.shape, 1)
    summed = jnp.sum(jnp.where(classes < CLASSES, jnp.exp(logits), 0.0), axis=1, keepdims=True)
    picked = jnp.sum(jnp.where(classes == tag_ref[...], logits, 0.0), axis=1, keepdims=True)
    losses = jnp.log(summed) - picked
    image = lax.broadcasted_iota(jnp.int32, losses.shape, 0)
    own_ref[...] = jnp.sum(jnp.where(image == mine_ref[0], losses, 0.0), axis=0, keepdims=True)
    mean_ref[...] = jnp.sum(losses, axis=0, keepdims=True) * (1.0 / IMAGES)


def call(kernel, outs, *args, scratch=(), smem=0, params=PARAMS):
    return pl.pallas_call(
        kernel,
        out_shape=[jax.ShapeDtypeStruct(s, d) for s, d in outs],
        in_specs=[SM] * smem + [VM] * (len(args) - smem),
        out_specs=[VM] * len(outs),
        scratch_shapes=list(scratch),
        compiler_params=params,
    )(*args)


def tile_frame(features, sy, sx):
    own = features[0]
    cols = jnp.where(sx == 0, own[:, TILE - HALO :], own[:, :HALO])
    rows = jnp.where(sy == 0, own[TILE - HALO :], own[:HALO])
    corner = jnp.where(sx == 0, rows[:, TILE - HALO :], rows[:, :HALO])
    cols = lax.ppermute(cols, "sx", [(0, 1), (1, 0)])
    rows = lax.ppermute(rows, "sy", [(0, 1), (1, 0)])
    corner = lax.ppermute(corner, ("sy", "sx"), [(i, 3 - i) for i in range(4)])
    right = jnp.concatenate([cols, corner], axis=0)
    right = jnp.where(sx == 1, jnp.concatenate([right[1:], right[:1]], axis=0), right)
    left = jnp.concatenate([own, rows], axis=0)
    return jnp.concatenate([left, right], axis=1).reshape(CELLS, FEAT)


def inside_image(sy, sx):
    cell = lax.broadcasted_iota(jnp.int32, (CELLS, 2 * MID), 0)
    col = cell % SIDE
    row = ((cell + jnp.where((sx == 1) & (col > TILE), SIDE, 0)) // SIDE) % SIDE
    inside = (row != SIDE - 1 - 3 * sy) & (col != SIDE - 1 - 3 * sx)
    return inside.astype(jnp.float32)


def exchange(copies, axes):
    rows = lax.all_to_all(copies, axes, 0, 0, tiled=True)
    return rows if rows.shape[1] > 1 else rows.reshape(rows.shape[0], -1)


def held_tiles(own, z4):
    fore, back = [(i, (i + 1) % 4) for i in range(4)], [((i + 1) % 4, i) for i in range(4)]
    half = CELLS // 2
    top, bottom = own[:half], own[half:]
    below = [lax.ppermute(v, "z4", fore) for v in (top, bottom)]
    above = [lax.ppermute(v, "z4", back) for v in (bottom, top)]

    def finish(after):
        low, high, after = lax.optimization_barrier((below[0], above[0], after))
        far = [lax.ppermute(low, "z4", fore), lax.ppermute(high, "z4", back)]
        return [above[1], high, *far, low, below[1]], after

    return finish


def per_device(
    features,
    labels,
    grid,
    w_reduce,
    w_spatial,
    w_expand,
    w_class,
    dir_reduce,
    dir_spatial,
    dir_expand,
    dir_class,
    gain_mid,
    shift_mid,
    gain_out,
    shift_out,
):
    z4, sy, sx = (lax.axis_index(a) for a in ("z4", "sy", "sx"))
    tile = 2 * sy + sx
    at = jnp.stack([sy, sx]).astype(jnp.int32)
    with jax.named_scope("filters"):
        (copies,) = call(
            filters_kernel,
            [((256, 8, 128), jnp.bfloat16)],
            grid, labels, tile.astype(jnp.int32).reshape(1),
            w_reduce[:, :, 0], jnp.transpose(dir_reduce[..., 0], (1, 0, 2)),
            w_spatial[..., 0], jnp.transpose(dir_spatial[..., 0], (1, 2, 3, 0, 4)),
            jnp.swapaxes(w_expand, 1, 2), jnp.swapaxes(dir_expand, 2, 3),
            w_class, dir_class,
            scratch=[
                pltpu.VMEM((ROWS, MID), jnp.float32),
                pltpu.VMEM((24, 128), jnp.float32),
                pltpu.VMEM((16, 1024), jnp.float32),
                pltpu.VMEM((64, 256), jnp.float32),
            ],
            smem=3,
            params=pltpu.CompilerParams(),
        )
        small = lax.ppermute(copies[0, 7:], "sx", [(0, 1), (1, 0)])
        features, small = lax.optimization_barrier((features, small))
        at = at + small[0, :2].astype(jnp.int32)
        every = lax.all_to_all(copies, ALL, 0, 0, tiled=True)

    with jax.named_scope("halo"):
        own = tile_frame(features, sy, sx)
        finish = held_tiles(own, z4)

    with jax.named_scope("reduce"):
        first = every.reshape(64, TILES, 8, 128)[:, 0, 2:4, :].reshape(MID, FEAT)
        (sent,) = call(reduce_kernel, [((256, 1, 128), jnp.float32)], own, first)
        later = (every, grid, gain_mid, shift_mid, gain_out, shift_out, at, sent)
        every, point, gain_mid, shift_mid, gain_out, shift_out, at, _ = lax.optimization_barrier(later)
        inside = inside_image(at[0], at[1])
        expand = every[:, :2, :].reshape(256, 256)
        flat = every[:, 2:7, :].reshape(64, FLAT * MID)

    with jax.named_scope("class"):
        rows = expand[:, 3 * MID :]
        high, low = (rows[::TILES, 3 * CLASS_PART + k].astype(jnp.int32) for k in range(2))
        table = high * 32 + low
        tags = table.reshape(4, 16).T.reshape(IMAGES)
        raw = rows[:, : 3 * CLASS_PART].astype(jnp.float32).reshape(FEAT, 3, CLASS_PART)
        norms = jnp.sum(raw * raw, axis=0)
        base = jnp.sqrt(norms[0])
        alpha = (2.0 * point.astype(jnp.float32) + 1.0 - GRID) / GRID
        p_class = raw[:, 0]
        for k in range(2):
            p_class = p_class + alpha[k] * (base / jnp.sqrt(norms[k + 1] + EPS_NORM)) * raw[:, k + 1]
        p_class = p_class.astype(jnp.bfloat16).astype(jnp.float32).T.reshape(2 * CLASS_PART, 128)

    row = lambda v: v.reshape(1, -1)
    mids = [[(row(gain_mid[b, k]), row(shift_mid[b, k])) for k in range(2)] for b in range(BLOCKS)]
    outs = [(row(gain_out[b]), row(shift_out[b])) for b in range(BLOCKS)]
    place = z4.astype(jnp.int32).reshape(1)
    parts = exchange(sent, ALL)
    pieces, after = finish((expand, flat, p_class, tags, inside, mids, outs))
    expand, flat, p_class, tags, inside, mids, outs = after
    mine = HELD * lax.axis_index(("z2", "y", "xh")) + z4
    mine = mine.astype(jnp.int32).reshape(1)
    early = (parts, expand, flat, p_class, tags, inside, mids, outs, place, mine)
    parts, expand, flat, p_class, tags, inside, mids, outs, place, mine = lax.optimization_barrier(early)
    pairs_of = lambda kind: ((PAIRS * CELLS, 2 * MID), kind)
    held = ((HELD * CELLS, FEAT), jnp.bfloat16)
    narrow, wide = ((64, 8, 128), jnp.bfloat16), ((64, 16, 128), jnp.bfloat16)
    spans = [(0, 6), (6, 11), (11, 16), (16, 22), (22, 27), (27, 32)]
    received = []
    for b in range(BLOCKS):
        with jax.named_scope(f"block_{b}"):
            if b == 0:
                (sent,) = call(
                    first_own_kernel, [((256, 1, 128), jnp.float32)],
                    parts, own, *mids[0][0], inside, flat,
                )
                x, c, sent = call(
                    functools.partial(first_expand_kernel, spans.pop(0)), [held, pairs_of(jnp.bfloat16), wide],
                    place, parts, exchange(sent, ALL), own, *pieces, *mids[0][0], *mids[0][1],
                    inside, flat, expand, p_class, smem=1,
                )
                parts = exchange(sent, GROUP)
                received.append((parts, 10))
            else:
                y2, sent = call(
                    functools.partial(spatial_kernel, b, spans.pop(0)), [pairs_of(jnp.float32), narrow],
                    parts, y1, *mids[b][0], inside, flat, p_class,
                )
                parts = exchange(sent, GROUP)
                received.append((parts, 3))
                last = b == BLOCKS - 1
                c, sent = call(
                    functools.partial(expand_kernel, b, None if last else spans.pop(0)),
                    [pairs_of(jnp.bfloat16), ((64, 4, 128), jnp.float32) if last else wide],
                    parts, y2, *mids[b][1], expand, *([] if last else [p_class]),
                )
                parts = exchange(sent, GROUP)
                if not last:
                    received.append((parts, 10))
            args = (parts, c, *outs[b], x, expand)
            if b < BLOCKS - 1:
                x, y1, sent = call(
                    functools.partial(block_kernel, b, spans.pop(0)), [held, pairs_of(jnp.float32), narrow],
                    *args, flat, p_class,
                )
                parts = exchange(sent, GROUP)
                received.append((parts, 3))
            else:
                section, sent = call(
                    functools.partial(last_kernel, b),
                    [((TILE, TILE, FEAT), jnp.bfloat16), ((64, 8, 128), jnp.float32)],
                    place, *args, smem=1,
                )
    with jax.named_scope("loss"):
        pooled = exchange(sent, GROUP).reshape(16, TILES, HELD, FEAT)
        pooled = (jnp.sum(pooled, axis=1) / (OWN * TILES)).astype(jnp.bfloat16).reshape(IMAGES, FEAT)
        arrays, _ = lax.optimization_barrier(([v for v, _ in received], sent))
        arrays = [v[:, start:] for v, (_, start) in zip(arrays, received)]
        classes = jnp.concatenate(arrays, axis=1).reshape(64 * CLASS_PART, FEAT)
        image_loss, mean_loss = call(
            loss_kernel, [((1, 1), jnp.float32)] * 2, mine, pooled, classes, tags.reshape(IMAGES, 1), smem=1
        )
    return section[None], image_loss.reshape(1), mean_loss.reshape(())


def solution(mesh):
    split = Mesh(
        mesh.devices.reshape(4, 2, 4, 2, mesh.shape["sy"], mesh.shape["sx"]), ALL
    )
    tiles = P(DP, "sy", "sx", None)
    return jax.shard_map(
        per_device,
        mesh=split,
        in_specs=(
            tiles,
            P(DP),
            P(),
            P(None, None, DP),
            P(None, None, None, None, DP),
            P(None, None, DP),
            P(DP, None),
            P(None, None, None, DP),
            P(None, None, None, None, None, DP),
            P(None, None, None, DP),
            P(None, DP, None),
            P(),
            P(),
            P(),
            P(),
        ),
        out_specs=(tiles, P(DP), P()),
        check_vma=False,
    )
```

```python
import functools

import jax
import jax.numpy as jnp
from jax import lax
from jax.experimental import pallas as pl
from jax.experimental.pallas import tpu as pltpu
from jax.sharding import Mesh
from jax.sharding import PartitionSpec as P

BLOCKS = 3
GRID = 50
EPS_NORM = 1e-06
EPS_BN = 1e-05
FEAT = 256
MID = 64
CLASSES = 1000
TILE = 28
OWN = TILE * TILE
SIDE = 32
CELLS = SIDE * SIDE
OWN_ROWS = TILE * SIDE
HALO = SIDE - TILE
DP = ("z4", "z2", "y", "xh")
GROUP = ("z2", "y", "xh", "sy", "sx")
ALL = ("z4",) + GROUP
TILES = 4
HELD = 4
PAIRS = HELD // 2
IMAGES = 64
CLASS_PART = 16

ROWS = 56
FLAT = 40

PARAMS = pltpu.CompilerParams(vmem_limit_bytes=16 * 1024 * 1024)
VM = pl.BlockSpec(memory_space=pltpu.VMEM)
SM = pl.BlockSpec(memory_space=pltpu.SMEM)


def dot_t(left, right):
    return lax.dot_general(
        left, right, (((1,), (1,)), ((), ())), preferred_element_type=jnp.float32
    )


def tile_moments(y):
    cells = y[:OWN_ROWS].reshape(TILE, SIDE, y.shape[1])
    mean = jnp.sum(jnp.sum(cells, axis=0)[:TILE], axis=0, keepdims=True) * (1.0 / OWN)
    off = cells - mean[None]
    return mean, jnp.sum(jnp.sum(off * off, axis=0)[:TILE], axis=0, keepdims=True)


def halves(pair):
    return [pair[:, :MID], pair[:, MID:]]


def merged(means, squares, cells):
    mean = functools.reduce(jnp.add, means) * (1.0 / len(means))
    total = functools.reduce(jnp.add, squares)
    for m in means:
        total = total + cells * ((m - mean) * (m - mean))
    return mean, total


def received_moments(parts):
    if parts.dtype == jnp.float32:
        return parts
    v = parts.astype(jnp.float32)
    if v.shape[1] == 8:
        return v + pltpu.roll(v, 7, 1) + pltpu.roll(v, 6, 1)
    upper, lower = v[:, :8], v[:, 8:]
    lower = jnp.where(lax.broadcasted_iota(jnp.int32, lower.shape, 1) < 2, lower, 0.0)
    return upper + pltpu.roll(upper, 4, 1) + lower


def normalizer(parts, gain, shift, cells, pairs=False, wide=False):
    parts = received_moments(parts)
    count = parts.shape[0]
    one_row = parts.ndim == 2
    total = jnp.sum(parts, axis=0, keepdims=one_row)
    off = parts - (total * (1.0 / count) if one_row else (total * (1.0 / count))[None])
    spread = jnp.sum(off * off, axis=0, keepdims=one_row)
    if wide:
        flat = lambda v: jnp.concatenate([v[:1], v[1:2]], axis=1)
        mean, squares, spread = flat(total), flat(total[2:4]), flat(spread)
    else:
        mean, squares, spread = total[:1, :MID], total[:1, MID:], spread[:1, :MID]
    mean = mean * (1.0 / count)
    scale = lax.rsqrt((squares + cells * spread) * (1.0 / (cells * count)) + EPS_BN) * gain
    if pairs:
        mean, scale, shift = (jnp.concatenate([v, v], axis=1) for v in (mean, scale, shift))
    return lambda y: (y - mean) * scale + shift


def send(out_ref, row):
    for k in range(out_ref.shape[1]):
        piece = row[:, 128 * k : 128 * (k + 1)].reshape(1, 1, 128)
        out_ref[:, k : k + 1, :] = jnp.broadcast_to(piece, (out_ref.shape[0], 1, 128))


def send_moments(out_ref, tiles, extra=None):
    mean, squares = merged([t[0] for t in tiles], [t[1] for t in tiles], OWN)
    row = jnp.concatenate([mean, squares], axis=1)
    if extra is None:
        return send(out_ref, row)
    rows = [row[:, 128 * k : 128 * (k + 1)] for k in range(row.shape[1] // 128)]
    left = rows[0] if len(rows) == 1 else jnp.concatenate(rows, axis=0)
    pieces = []
    for k in range(3):
        if k == 2:
            left = left[: max(1, len(rows) // 2)]
        piece = left.astype(jnp.bfloat16).astype(jnp.float32)
        pieces.append(piece)
        left = left - piece
    block = jnp.concatenate(pieces + [extra], axis=0).astype(jnp.bfloat16)
    out_ref[...] = jnp.broadcast_to(block[None], (out_ref.shape[0], *block.shape))


def pair_moments(pair):
    mean, squares = tile_moments(pair)
    return list(zip(halves(mean), halves(squares)))


def filters_kernel(
    grid_ref, label_ref, tile_ref, wr_ref, dr_ref, ws_ref, ds_ref, we_ref, de_ref, wc_ref, dc_ref, out_ref, small_ref, rows, flat, classes, sent
):
    alpha = [(2.0 * grid_ref[k].astype(jnp.float32) + 1.0 - GRID) / GRID for k in range(2)]
    wide = lambda v: v.astype(jnp.float32)

    def filters(base, directions, axes):
        square = lambda v: jnp.sum(v * v, axis=axes, keepdims=True)
        length = jnp.sqrt(square(base))
        value = base
        for k in range(2):
            value = value + alpha[k] * (length / jnp.sqrt(square(directions[k]) + EPS_NORM)) * directions[k]
        return value

    rows[...] = jnp.zeros_like(rows)
    small_ref[...] = jnp.zeros_like(small_ref)
    both = wide(dr_ref[...])
    reduce = filters(wide(wr_ref[...]), [both[:, k, :] for k in range(2)], 1)
    for b in range(BLOCKS):
        for q in range(4):
            rows[4 * b + q : 4 * b + q + 1, :] = reduce[b : b + 1, MID * q : MID * (q + 1)]
        both = wide(ds_ref[b])
        spatial = filters(wide(ws_ref[b]), [both[:, :, k, :] for k in range(2)], (0, 1, 2))
        for i in range(3):
            rows[12 + 9 * b + 3 * i : 15 + 9 * b + 3 * i, :] = spatial[i]
        expand = filters(wide(we_ref[b]), [wide(de_ref[k, b]) for k in range(2)], 1)
        for k in range(4):
            rows[FLAT + 3 * k + b : FLAT + 3 * k + b + 1, :] = expand[k : k + 1]
    flat[0:20, :] = jnp.concatenate([rows[pl.ds(h, 20, stride=2), :] for h in range(2)], axis=1)
    tile = tile_ref[0]
    quarter = flat[pl.ds(5 * tile, 5), :]

    classes[...] = jnp.zeros_like(classes)
    classes[0:4, :CLASSES] = wide(wc_ref[...])
    for k in range(2):
        classes[4 + 4 * k : 8 + 4 * k, :CLASSES] = wide(dc_ref[k])
    sent[...] = jnp.zeros_like(sent)
    for b in range(BLOCKS):
        sent[:, MID * b : MID * (b + 1)] = jnp.broadcast_to(rows[pl.ds(FLAT + 3 * tile + b, 1), :], (64, MID))
    for a in range(3):
        row = classes[pl.ds(4 * a + tile, 1), :]
        at = 3 * MID + CLASS_PART * a
        for g in range(64):
            sent[g : g + 1, at : at + CLASS_PART] = row[:, CLASS_PART * g : CLASS_PART * (g + 1)]
    at = 3 * MID + 3 * CLASS_PART
    label = label_ref[0]
    sent[:, at : at + 1] = jnp.full((64, 1), wide(label >> 5), jnp.float32)
    sent[:, at + 1 : at + 2] = jnp.full((64, 1), wide(label & 31), jnp.float32)
    pieces = [sent[:, :128].reshape(64, 1, 128), sent[:, 128:].reshape(64, 1, 128)]
    pieces += [jnp.broadcast_to(quarter[None], (64, 5, 128)), jnp.zeros((64, 1, 128), jnp.float32)]
    copies = jnp.concatenate(pieces, axis=1).astype(jnp.bfloat16)
    for z in range(4):
        out_ref[64 * z : 64 * (z + 1)] = copies


def reduce_kernel(x_ref, w_ref, out_ref):
    send_moments(out_ref, [tile_moments(dot_t(x_ref[...], w_ref[...]))])


def reduced_pair(first, second, w):
    zero = jnp.zeros_like(w)
    return dot_t(first, jnp.concatenate([w, zero], axis=0)) + dot_t(
        second, jnp.concatenate([zero, w], axis=0)
    )


def tile_at(k):
    return slice(CELLS * k, CELLS * (k + 1))


def reduce_of(flat_ref, block):
    return flat_ref[:, FEAT * block : FEAT * (block + 1)]


def spatial_of(flat_ref, block):
    start = FEAT * BLOCKS + 9 * MID * block
    taps = [flat_ref[:, start + MID * t : start + MID * (t + 1)] for t in range(9)]
    zero = jnp.zeros_like(taps[0])
    rows = []
    for i in range(3):
        rows.append(jnp.concatenate([v for t in taps[3 * i : 3 * i + 3] for v in (t, zero)], axis=1))
        rows.append(jnp.concatenate([v for t in taps[3 * i : 3 * i + 3] for v in (zero, t)], axis=1))
    return jnp.concatenate(rows, axis=0)


def expand_of(expand_ref, block):
    w = expand_ref[:, MID * block : MID * (block + 1)]
    zero = jnp.zeros_like(w)
    return [jnp.concatenate(v, axis=1) for v in ((w, zero), (zero, w))]


def convolved(y, norm, inside, taps):
    a = jnp.maximum(norm(y), 0.0) * inside
    sides = [v.astype(jnp.bfloat16) for v in (pltpu.roll(a, 1, 0), a, pltpu.roll(a, CELLS - 1, 0))]
    each = dot_t(jnp.concatenate(sides, axis=1), taps)
    above, here, below = (each[:, 2 * MID * i : 2 * MID * (i + 1)] for i in range(3))
    above = jnp.concatenate([above[CELLS - SIDE :], above[: CELLS - SIDE]], axis=0)
    below = jnp.concatenate([below[SIDE:], below[:SIDE]], axis=0)
    return above + here + below


def first_own_kernel(parts_ref, x_ref, gain_ref, shift_ref, inside_ref, flat_ref, out_ref):
    norm = normalizer(parts_ref[...], gain_ref[...], shift_ref[...], OWN, True)
    y = reduced_pair(x_ref[...], x_ref[...], reduce_of(flat_ref, 0))
    y2 = convolved(y, norm, inside_ref[...], spatial_of(flat_ref, 0))
    send_moments(out_ref, pair_moments(y2)[:1])


def expanded(c, pair_weights, tiles):
    for w in pair_weights:
        tiles.append(tile_moments(dot_t(c[:OWN_ROWS], w)))


def first_expand_kernel(
    span, at_ref, parts_ref, parts2_ref, own_ref, *refs
):
    pieces, (gain_ref, shift_ref, gain2_ref, shift2_ref, inside_ref, flat_ref, expand_ref, extra_ref) = refs[:6], refs[6:14]
    x_ref, c_ref, out_ref = refs[14:]
    half = CELLS // 2
    for off in range(HELD):
        start = lax.rem(at_ref[0] + off, HELD) * CELLS
        for h in range(2):
            piece = own_ref[half * h : half * (h + 1), :] if off == 0 else pieces[2 * (off - 1) + h][...]
            x_ref[pl.ds(pl.multiple_of(start + half * h, half), half), :] = piece
    norm = normalizer(parts_ref[...], gain_ref[...], shift_ref[...], OWN, True)
    norm2 = normalizer(parts2_ref[...], gain2_ref[...], shift2_ref[...], OWN, True)
    taps, weights = spatial_of(flat_ref, 0), expand_of(expand_ref, 0)
    tiles = []
    for p in range(PAIRS):
        y = reduced_pair(x_ref[tile_at(2 * p), :], x_ref[tile_at(2 * p + 1), :], reduce_of(flat_ref, 0))
        y2 = convolved(y, norm, inside_ref[...], taps)
        c = jnp.maximum(norm2(y2), 0.0).astype(jnp.bfloat16)
        c_ref[tile_at(p), :] = c
        expanded(c, weights, tiles)
    send_moments(out_ref, tiles, extra_ref[span[0] : span[1], :])


def spatial_kernel(block, span, parts_ref, y_ref, gain_ref, shift_ref, inside_ref, flat_ref, extra_ref, y2_ref, out_ref):
    norm = normalizer(parts_ref[...], gain_ref[...], shift_ref[...], HELD * OWN, True)
    taps = spatial_of(flat_ref, block)
    tiles = []
    for p in range(PAIRS):
        y2 = convolved(y_ref[tile_at(p), :], norm, inside_ref[...], taps)
        y2_ref[tile_at(p), :] = y2
        tiles += pair_moments(y2)
    send_moments(out_ref, tiles, extra_ref[span[0] : span[1], :])


def expand_kernel(block, span, parts_ref, y_ref, gain_ref, shift_ref, expand_ref, *rest):
    extra = rest[0][span[0] : span[1], :] if span else None
    c_ref, out_ref = rest[-2:]
    norm = normalizer(parts_ref[...], gain_ref[...], shift_ref[...], HELD * OWN, True)
    weights = expand_of(expand_ref, block)
    tiles = []
    for p in range(PAIRS):
        c = jnp.maximum(norm(y_ref[tile_at(p), :]), 0.0).astype(jnp.bfloat16)
        c_ref[tile_at(p), :] = c
        expanded(c, weights, tiles)
    send_moments(out_ref, tiles, extra)


def block_kernel(block, span, parts_ref, c_ref, gain_ref, shift_ref, x_ref, expand_ref, flat_ref, extra_ref, new_ref, y1_ref, out_ref):
    norm = normalizer(parts_ref[...], gain_ref[...], shift_ref[...], HELD * OWN, wide=True)
    weights = expand_of(expand_ref, block)
    tiles = []
    for p in range(PAIRS):
        pair = []
        for h in range(2):
            y = dot_t(c_ref[tile_at(p), :], weights[h])
            x = x_ref[tile_at(2 * p + h), :].astype(jnp.float32)
            new = jnp.maximum(x + norm(y), 0.0).astype(jnp.bfloat16)
            new_ref[tile_at(2 * p + h), :] = new
            pair.append(new)
        y1 = reduced_pair(*pair, reduce_of(flat_ref, block + 1))
        y1_ref[tile_at(p), :] = y1
        tiles += pair_moments(y1)
    send_moments(out_ref, tiles, extra_ref[span[0] : span[1], :])


def last_kernel(block, at_ref, parts_ref, c_ref, gain_ref, shift_ref, x_ref, expand_ref, new_ref, out_ref):
    norm = normalizer(parts_ref[...], gain_ref[...], shift_ref[...], HELD * OWN, wide=True)
    weights = expand_of(expand_ref, block)
    sums = []
    for k in range(HELD):
        c = c_ref[tile_at(k // 2), :][:OWN_ROWS]
        y = dot_t(c, weights[k % 2])
        top = x_ref[tile_at(k), :][:OWN_ROWS].astype(jnp.float32) + norm(y)
        new = jnp.maximum(top, 0.0).astype(jnp.bfloat16)

        @pl.when(at_ref[0] == k)
        def _():
            for row in range(TILE):
                new_ref[row] = new[SIDE * row : SIDE * row + TILE]

        by_col = jnp.sum(new.astype(jnp.float32).reshape(TILE, SIDE, FEAT), axis=0)
        sums.append(jnp.sum(by_col[:TILE], axis=0, keepdims=True))
    send(out_ref, jnp.concatenate(sums, axis=1))


def loss_kernel(mine_ref, pooled_ref, class_ref, tag_ref, own_ref, mean_ref):
    logits = dot_t(pooled_ref[...], class_ref[...])
    classes = lax.broadcasted_iota(jnp.int32, logits.shape, 1)
    summed = jnp.sum(jnp.where(classes < CLASSES, jnp.exp(logits), 0.0), axis=1, keepdims=True)
    picked = jnp.sum(jnp.where(classes == tag_ref[...], logits, 0.0), axis=1, keepdims=True)
    losses = jnp.log(summed) - picked
    image = lax.broadcasted_iota(jnp.int32, losses.shape, 0)
    own_ref[...] = jnp.sum(jnp.where(image == mine_ref[0], losses, 0.0), axis=0, keepdims=True)
    mean_ref[...] = jnp.sum(losses, axis=0, keepdims=True) * (1.0 / IMAGES)


def call(kernel, outs, *args, scratch=(), smem=0, params=PARAMS):
    return pl.pallas_call(
        kernel,
        out_shape=[jax.ShapeDtypeStruct(s, d) for s, d in outs],
        in_specs=[SM] * smem + [VM] * (len(args) - smem),
        out_specs=[VM] * len(outs),
        scratch_shapes=list(scratch),
        compiler_params=params,
    )(*args)


def tile_frame(features, sy, sx):
    own = features[0]
    cols = jnp.where(sx == 0, own[:, TILE - HALO :], own[:, :HALO])
    rows = jnp.where(sy == 0, own[TILE - HALO :], own[:HALO])
    corner = jnp.where(sx == 0, rows[:, TILE - HALO :], rows[:, :HALO])
    cols = lax.ppermute(cols, "sx", [(0, 1), (1, 0)])
    rows = lax.ppermute(rows, "sy", [(0, 1), (1, 0)])
    corner = lax.ppermute(corner, ("sy", "sx"), [(i, 3 - i) for i in range(4)])
    right = jnp.concatenate([cols, corner], axis=0)
    right = jnp.where(sx == 1, jnp.concatenate([right[1:], right[:1]], axis=0), right)
    left = jnp.concatenate([own, rows], axis=0)
    return jnp.concatenate([left, right], axis=1).reshape(CELLS, FEAT)


def inside_image(sy, sx):
    cell = lax.broadcasted_iota(jnp.int32, (CELLS, 2 * MID), 0)
    col = cell % SIDE
    row = ((cell + jnp.where((sx == 1) & (col > TILE), SIDE, 0)) // SIDE) % SIDE
    inside = (row != SIDE - 1 - 3 * sy) & (col != SIDE - 1 - 3 * sx)
    return inside.astype(jnp.float32)


def exchange(copies, axes):
    rows = lax.all_to_all(copies, axes, 0, 0, tiled=True)
    return rows if rows.shape[1] > 1 else rows.reshape(rows.shape[0], -1)


def held_tiles(own, z4):
    fore, back = [(i, (i + 1) % 4) for i in range(4)], [((i + 1) % 4, i) for i in range(4)]
    half = CELLS // 2
    top, bottom = own[:half], own[half:]
    below = [lax.ppermute(v, "z4", fore) for v in (top, bottom)]
    above = [lax.ppermute(v, "z4", back) for v in (bottom, top)]

    def finish(after):
        low, high, after = lax.optimization_barrier((below[0], above[0], after))
        far = [lax.ppermute(low, "z4", fore), lax.ppermute(high, "z4", back)]
        return [above[1], high, *far, low, below[1]], after

    return finish


def per_device(
    features,
    labels,
    grid,
    w_reduce,
    w_spatial,
    w_expand,
    w_class,
    dir_reduce,
    dir_spatial,
    dir_expand,
    dir_class,
    gain_mid,
    shift_mid,
    gain_out,
    shift_out,
):
    z4, sy, sx = (lax.axis_index(a) for a in ("z4", "sy", "sx"))
    tile = 2 * sy + sx
    at = jnp.stack([sy, sx]).astype(jnp.int32)
    with jax.named_scope("filters"):
        copies, small = call(
            filters_kernel,
            [((256, 8, 128), jnp.bfloat16), ((1, 128), jnp.float32)],
            grid, labels, tile.astype(jnp.int32).reshape(1),
            w_reduce[:, :, 0], jnp.transpose(dir_reduce[..., 0], (1, 0, 2)),
            w_spatial[..., 0], jnp.transpose(dir_spatial[..., 0], (1, 2, 3, 0, 4)),
            jnp.swapaxes(w_expand, 1, 2), jnp.swapaxes(dir_expand, 2, 3),
            w_class, dir_class,
            scratch=[
                pltpu.VMEM((ROWS, MID), jnp.float32),
                pltpu.VMEM((24, 128), jnp.float32),
                pltpu.VMEM((16, 1024), jnp.float32),
                pltpu.VMEM((64, 256), jnp.float32),
            ],
            smem=3,
            params=pltpu.CompilerParams(),
        )
        small = lax.ppermute(small, "sx", [(0, 1), (1, 0)])
        features, small = lax.optimization_barrier((features, small))
        at = at + small[0, :2].astype(jnp.int32)
        every = lax.all_to_all(copies, ALL, 0, 0, tiled=True)

    with jax.named_scope("halo"):
        own = tile_frame(features, sy, sx)
        finish = held_tiles(own, z4)

    with jax.named_scope("reduce"):
        first = every.reshape(64, TILES, 8, 128)[:, 0, 2:4, :].reshape(MID, FEAT)
        (sent,) = call(reduce_kernel, [((256, 1, 128), jnp.float32)], own, first)
        later = (every, grid, gain_mid, shift_mid, gain_out, shift_out, at, sent)
        every, point, gain_mid, shift_mid, gain_out, shift_out, at, _ = lax.optimization_barrier(later)
        inside = inside_image(at[0], at[1])
        expand = every[:, :2, :].reshape(256, 256)
        flat = every[:, 2:7, :].reshape(64, FLAT * MID)

    with jax.named_scope("class"):
        rows = expand[:, 3 * MID :]
        high, low = (rows[::TILES, 3 * CLASS_PART + k].astype(jnp.int32) for k in range(2))
        table = high * 32 + low
        tags = table.reshape(4, 16).T.reshape(IMAGES)
        raw = rows[:, : 3 * CLASS_PART].astype(jnp.float32).reshape(FEAT, 3, CLASS_PART)
        norms = jnp.sum(raw * raw, axis=0)
        base = jnp.sqrt(norms[0])
        alpha = (2.0 * point.astype(jnp.float32) + 1.0 - GRID) / GRID
        p_class = raw[:, 0]
        for k in range(2):
            p_class = p_class + alpha[k] * (base / jnp.sqrt(norms[k + 1] + EPS_NORM)) * raw[:, k + 1]
        p_class = p_class.astype(jnp.bfloat16).astype(jnp.float32).T.reshape(2 * CLASS_PART, 128)

    row = lambda v: v.reshape(1, -1)
    mids = [[(row(gain_mid[b, k]), row(shift_mid[b, k])) for k in range(2)] for b in range(BLOCKS)]
    outs = [(row(gain_out[b]), row(shift_out[b])) for b in range(BLOCKS)]
    place = z4.astype(jnp.int32).reshape(1)
    parts = exchange(sent, ALL)
    pieces, after = finish((expand, flat, p_class, tags, inside, mids, outs))
    expand, flat, p_class, tags, inside, mids, outs = after
    mine = HELD * lax.axis_index(("z2", "y", "xh")) + z4
    mine = mine.astype(jnp.int32).reshape(1)
    early = (parts, expand, flat, p_class, tags, inside, mids, outs, place, mine)
    parts, expand, flat, p_class, tags, inside, mids, outs, place, mine = lax.optimization_barrier(early)
    pairs_of = lambda kind: ((PAIRS * CELLS, 2 * MID), kind)
    held = ((HELD * CELLS, FEAT), jnp.bfloat16)
    narrow, wide = ((64, 8, 128), jnp.bfloat16), ((64, 16, 128), jnp.bfloat16)
    spans = [(0, 6), (6, 11), (11, 16), (16, 22), (22, 27), (27, 32)]
    received = []
    for b in range(BLOCKS):
        with jax.named_scope(f"block_{b}"):
            if b == 0:
                (sent,) = call(
                    first_own_kernel, [((256, 1, 128), jnp.float32)],
                    parts, own, *mids[0][0], inside, flat,
                )
                x, c, sent = call(
                    functools.partial(first_expand_kernel, spans.pop(0)), [held, pairs_of(jnp.bfloat16), wide],
                    place, parts, exchange(sent, ALL), own, *pieces, *mids[0][0], *mids[0][1],
                    inside, flat, expand, p_class, smem=1,
                )
                parts = exchange(sent, GROUP)
                received.append((parts, 10))
            else:
                y2, sent = call(
                    functools.partial(spatial_kernel, b, spans.pop(0)), [pairs_of(jnp.float32), narrow],
                    parts, y1, *mids[b][0], inside, flat, p_class,
                )
                parts = exchange(sent, GROUP)
                received.append((parts, 3))
                last = b == BLOCKS - 1
                c, sent = call(
                    functools.partial(expand_kernel, b, None if last else spans.pop(0)),
                    [pairs_of(jnp.bfloat16), ((64, 4, 128), jnp.float32) if last else wide],
                    parts, y2, *mids[b][1], expand, *([] if last else [p_class]),
                )
                parts = exchange(sent, GROUP)
                if not last:
                    received.append((parts, 10))
            args = (parts, c, *outs[b], x, expand)
            if b < BLOCKS - 1:
                x, y1, sent = call(
                    functools.partial(block_kernel, b, spans.pop(0)), [held, pairs_of(jnp.float32), narrow],
                    *args, flat, p_class,
                )
                parts = exchange(sent, GROUP)
                received.append((parts, 3))
            else:
                section, sent = call(
                    functools.partial(last_kernel, b),
                    [((TILE, TILE, FEAT), jnp.bfloat16), ((64, 8, 128), jnp.float32)],
                    place, *args, smem=1,
                )
    with jax.named_scope("loss"):
        pooled = exchange(sent, GROUP).reshape(16, TILES, HELD, FEAT)
        pooled = (jnp.sum(pooled, axis=1) / (OWN * TILES)).astype(jnp.bfloat16).reshape(IMAGES, FEAT)
        arrays, _ = lax.optimization_barrier(([v for v, _ in received], sent))
        arrays = [v[:, start:] for v, (_, start) in zip(arrays, received)]
        classes = jnp.concatenate(arrays, axis=1).reshape(64 * CLASS_PART, FEAT)
        image_loss, mean_loss = call(
            loss_kernel, [((1, 1), jnp.float32)] * 2, mine, pooled, classes, tags.reshape(IMAGES, 1), smem=1
        )
    return section[None], image_loss.reshape(1), mean_loss.reshape(())


def solution(mesh):
    split = Mesh(
        mesh.devices.reshape(4, 2, 4, 2, mesh.shape["sy"], mesh.shape["sx"]), ALL
    )
    tiles = P(DP, "sy", "sx", None)
    return jax.shard_map(
        per_device,
        mesh=split,
        in_specs=(
            tiles,
            P(DP),
            P(),
            P(None, None, DP),
            P(None, None, None, None, DP),
            P(None, None, DP),
            P(DP, None),
            P(None, None, None, DP),
            P(None, None, None, None, None, DP),
            P(None, None, None, DP),
            P(None, DP, None),
            P(),
            P(),
            P(),
            P(),
        ),
        out_specs=(tiles, P(DP), P()),
        check_vma=False,
    )
```
